128 devices in a mesh: dp: 64 (over y, z_hi, x, core), tower: 2 (over z_lo).
Axes of the slice: x: 4, y: 4, z: 4 (z_hi: 2, z_lo: 2; z = z_hi * 2 + z_lo), core: 2. Of those that a mesh axis runs over, the one named last changes fastest.
Arguments:
- image: bfloat16 [65536, 1152], P('dp', 'tower'), may hold values from -0.19921875 to 0.19921875
- text: bfloat16 [65536, 1152], P('dp', 'tower'), may hold values from -0.19921875 to 0.19921875
- scale: float32 [], replicated, may hold values from 3 to 8
- bias: float32 [], replicated, may hold values from -3 to -1
- table: int32 [3, 64], replicated, may hold values from 0 to 63, as said below
- labels: int32 [64, 1024], P('dp'), may hold values from 0 to 1023, each once within a row
Outputs:
- image_grad: float32 [65536, 1152], P('dp', 'tower')
- text_grad: float32 [65536, 1152], P('dp', 'tower')
The draws below stay inside these ranges and needn't reach their ends.
Inputs may be any that keep to these rules, and one draw needn't show every extreme that they name: For every round k there is a bit number b_k with table[k, d] = d xor 2^b_k for every d; the b_k of the 3 rounds are distinct. Each block's row of labels holds every number of 0 to 1023 once.
All inputs are finite; a program needn't handle non-finite values.
Results may differ from the reference program's by a relative error of at most 0.0043.
Values may be sent and summed in bfloat16 or wider, within the bound.
A program may use at most 192 MiB of HBM per device.

```python
import jax
import jax.numpy as jnp
from jax import lax

D = 1152
ROWS = 1024
ROUNDS = 3
BATCH = 65536
N_DP = 64


def draw_table(key, part):
    key = jax.random.fold_in(key, 7)
    bit_count = int(N_DP).bit_length() - 1
    chosen = jax.random.permutation(key, bit_count)[:ROUNDS].astype(jnp.int32)
    masks = jnp.left_shift(jnp.ones_like(chosen), chosen)
    blocks = jnp.arange(N_DP, dtype=jnp.int32)
    return jnp.bitwise_xor(blocks[None, :], masks[:, None]).astype(jnp.int32)


def level_of(own_key, shape, shards, low, top_value):
    gain, own = 1.0, jax.random.fold_in(own_key, 6)
    for position, shards_of in shards:
        steps = jnp.exp(jax.random.uniform(jax.random.fold_in(own, position), (shards_of,), jnp.float32, low / len(shards), top_value / len(shards)))
        gain = gain * jnp.repeat(steps, shape[position] // shards_of).reshape([-1 if axis == position else 1 for axis in range(len(shape))])
    return gain


def noise(rng, extent, scale, most, cuts=(), kind=jnp.bfloat16):
    values = scale * jax.random.normal(rng, extent, jnp.float32)
    if cuts:
        values = values * level_of(rng, extent, cuts, -0.22, 0.18)
    return jnp.clip(values, -most, most).astype(kind)


def setup_inputs(seed: int = 0) -> dict:
    arg_keys = jax.random.split(jax.random.key(seed), 7)
    image = noise(arg_keys[0], (BATCH, D), 0.03, 0.19921875, ((0, 64), (1, 2)))
    text = noise(arg_keys[1], (BATCH, D), 0.03, 0.19921875, ((0, 64), (1, 2)))
    scale = jnp.clip(jax.random.uniform(arg_keys[2], (), jnp.float32, 3.0, 8.0), 3.0, 8.0)
    bias = jnp.clip(jax.random.uniform(arg_keys[3], (), jnp.float32, -3.0, -1.0), -3.0, -1.0)
    table = draw_table(jax.random.fold_in(arg_keys[6], 71), 0)
    labels = jax.vmap(lambda own: jax.random.permutation(own, ROWS))(jax.random.split(arg_keys[5], N_DP)).reshape((N_DP, ROWS)).astype(jnp.int32)
    return dict(image=image, text=text, scale=scale, bias=bias, table=table, labels=labels)


def normalize(rows):
    wide = rows.astype(jnp.float32)
    inverse = lax.rsqrt(lax.optimization_barrier(jnp.sum(wide * wide, axis=1, keepdims=True)) + 1e-06)
    return (wide * inverse, inverse)

def reference(image, text, scale, bias, table, labels):
    unit_image, inverse_image = normalize(image)
    unit_text, inverse_text = normalize(text)
    image_blocks = unit_image.astype(jnp.bfloat16).reshape(N_DP, ROWS, D)
    text_blocks = unit_text.astype(jnp.bfloat16).reshape(N_DP, ROWS, D)
    columns = jnp.arange(ROWS, dtype=jnp.int32)

    def one_block(block):
        own_image = image_blocks[block]
        own_text = text_blocks[block]
        partners = jnp.concatenate([jnp.full((1,), block, jnp.int32), table[:, block].astype(jnp.int32)])

        def add_tile(carry, partner):
            grad_image, grad_text = carry
            same = (partner == block).astype(jnp.float32)
            other_text = text_blocks[partner]
            other_image = image_blocks[partner]
            first = scale * jnp.dot(own_image, other_text.T, preferred_element_type=jnp.float32) + bias
            first_pos = same * (columns[None, :] == labels[block][:, None]).astype(jnp.float32)
            first_weight = (jax.nn.sigmoid(first) - first_pos).astype(jnp.bfloat16)
            grad_image = grad_image + jnp.dot(first_weight, other_text, preferred_element_type=jnp.float32)
            second = scale * jnp.dot(other_image, own_text.T, preferred_element_type=jnp.float32) + bias
            second_pos = same * (columns[None, :] == labels[partner][:, None]).astype(jnp.float32)
            second_weight = (jax.nn.sigmoid(second) - second_pos).astype(jnp.bfloat16)
            grad_text = grad_text + jnp.dot(second_weight.T, other_image, preferred_element_type=jnp.float32)
            return ((grad_image, grad_text), None)
        start = (jnp.zeros((ROWS, D), jnp.float32), jnp.zeros((ROWS, D), jnp.float32))
        (grad_image, grad_text), _ = lax.scan(add_tile, start, partners)
        return (scale * grad_image, scale * grad_text)
    normed_image_grad, normed_text_grad = lax.map(one_block, jnp.arange(N_DP, dtype=jnp.int32))
    normed_image_grad = normed_image_grad.reshape(N_DP * ROWS, D)
    normed_text_grad = normed_text_grad.reshape(N_DP * ROWS, D)
    image_along = lax.optimization_barrier(jnp.sum(unit_image * normed_image_grad, axis=1, keepdims=True))
    text_along = lax.optimization_barrier(jnp.sum(unit_text * normed_text_grad, axis=1, keepdims=True))
    image_grad = inverse_image * (normed_image_grad - unit_image * image_along)
    text_grad = inverse_text * (normed_text_grad - unit_text * text_along)
    return (image_grad, text_grad)
```

```python
from functools import partial
from itertools import combinations

import jax
import jax.numpy as jnp
from jax import lax
from jax.experimental import pallas as pl
from jax.experimental.pallas import tpu as pltpu
from jax.sharding import PartitionSpec as P

MESH = pl.DeviceIdType.MESH
BF = jnp.bfloat16
F32 = jnp.float32
CHUNK = 256
HALF = CHUNK // 2
PACKED = CHUNK + CHUNK // 8
NT = (((1,), (1,)), ((), ()))
BITS = 6
AXES = ((1, 2), (4, 5), (0, 3))


def tail_at(r):
    return pl.ds(CHUNK + r % 32, 16), pl.ds(128 * (r // 32), 128)


def low_lanes():
    return lax.broadcasted_iota(jnp.int32, (16, 128), 1) < 64


def merge_tails(low, first, second):
    return (
        jnp.where(low, first, pltpu.roll(second, 64, 1)),
        jnp.where(low, pltpu.roll(first, 64, 1), second),
    )


def rows_of(raw, slot, array, chunk, r, low):
    tails = [raw[slot, array, h, chunk, tail_at(r)[0], tail_at(r)[1]].astype(F32) for h in range(2)]
    tails = merge_tails(low, *tails)
    return [
        (
            raw[slot, array, 0, chunk, pl.ds(r + HALF * part, 16), :].astype(F32),
            raw[slot, array, 1, chunk, pl.ds(r + HALF * part, 16), :].astype(F32),
            tails[part],
        )
        for part in range(2)
    ]


def lane_sum(first, second, tails):
    total = first + second
    total = total[:, 0:128] + total[:, 128:256] + total[:, 256:384] + total[:, 384:512] + tails
    return jnp.sum(total, axis=1, keepdims=True)


def normalise(raw, slot, array, chunk, out, base):
    low = low_lanes()
    for r in range(0, HALF, 16):
        for part, (m0, m1, t) in enumerate(rows_of(raw, slot, array, chunk, r, low)):
            inverse = lax.rsqrt(lane_sum(m0 * m0, m1 * m1, t * t) + 1e-06)
            rows = pl.ds(base + r + HALF * part, 16)
            out[rows, 0:512] = (m0 * inverse).astype(BF)
            out[rows, 512:1024] = (m1 * inverse).astype(BF)
            out[rows, 1024:1152] = (t * inverse).astype(BF)


def flip(index, bit):
    return index + (1 - 2 * ((index // (1 << bit)) % 2)) * (1 << bit)


def kernel(
    bits, scalars, labels_in, text_in, image_in, text_out, image_out,
    raw, q, kn, acc, packed_out, landed, labels, label_column,
    swap_s, swap_r, link_s, link_r, core_s, core_r, relay_s, last_s, last_r, label_s, label_r,
):
    me, a = lax.axis_index("dp"), lax.axis_index("tower")
    c = me % 2
    other = (c - a) * (c - a)
    sibling = (me + 1 - 2 * c, a)
    across = (me, 1 - a)
    diagonal = (me + 1 - 2 * c, 1 - a)
    slots = range(1, len(bits) + 1)
    partner = {s: across if b == 0 else (flip(me, b), a) for s, b in zip(slots, bits)}
    relays = {}
    for near, far in AXES:
        if near in bits and far in bits:
            s_near, s_far = bits.index(near) + 1, bits.index(far) + 1
            device = (flip(me, far), 1 - a) if near == 0 else (flip(flip(me, near), far), a)
            relays[s_near] = (s_far, device)
    relayed = {far for far, _ in relays.values()}
    direct = [s for s in slots if s not in relayed]

    barrier = pltpu.get_barrier_semaphore()
    peers = [sibling, across, diagonal]
    peers += [partner[s] for s in direct if bits[s - 1] != 0] + [d for _, d in relays.values()]
    for peer in peers:
        pl.semaphore_signal(barrier, inc=1, device_id=peer, device_id_type=MESH)

    def remote(src, dst, send, recv, device):
        return pltpu.make_async_remote_copy(
            src_ref=src, dst_ref=dst, send_sem=send, recv_sem=recv, device_id=device, device_id_type=MESH
        )

    def swap_copy(array, chunk):
        return remote(
            raw.at[4, array, a, chunk], raw.at[0, array, a, chunk],
            swap_s.at[array, chunk], swap_r.at[array, chunk], (me - c + a, c),
        )

    def swap_wait(array, chunk):
        remote(
            raw.at[4, array, c, chunk], raw.at[0, array, c, chunk],
            swap_s.at[array, chunk], swap_r.at[array, chunk], (me - c + a, c),
        ).wait_recv()

    def link_copy(s, array, chunk):
        return remote(
            raw.at[0, array, c, chunk], raw.at[s, array, c, chunk],
            link_s.at[s - 1, array, chunk], link_r.at[s - 1, array, chunk], partner[s],
        )

    def core_copy(s, array, chunk, half):
        return remote(
            raw.at[s, array, half, chunk], raw.at[s, array, half, chunk],
            core_s.at[s, array, chunk], core_r.at[s, array, chunk], sibling,
        )

    def relay_copy(s, array, chunk):
        far, device = relays[s]
        return remote(
            raw.at[s, array, c, chunk], raw.at[far, array, c, chunk],
            relay_s.at[array, chunk], link_r.at[far - 1, array, chunk], device,
        )

    def fan_out(array, chunk):
        for s in direct:
            link_copy(s, array, chunk).start()
        core_copy(0, array, chunk, c).start()

    def pass_on(s, array, chunk):
        link_copy(s, array, chunk).wait_recv()
        if s in relays:
            relay_copy(s, array, chunk).start()
        core_copy(s, array, chunk, c).start()

    low = low_lanes()

    def pack(n, carry):
        array, chunk = n // 4, n % 4
        slot = 4 * other

        def one(src):
            row = pl.multiple_of(chunk * CHUNK, CHUNK)
            raw[slot, array, a, chunk, 0:CHUNK, :] = src[pl.ds(row, CHUNK), 0:512]
            for r in range(0, HALF, 16):
                pair = [src[pl.ds(row + r + HALF * part, 16), 512:576].astype(F32) for part in range(2)]
                raw[slot, array, a, chunk, tail_at(r)[0], tail_at(r)[1]] = jnp.concatenate(pair, axis=1).astype(BF)

        pl.when(array == 0)(partial(one, text_in))
        pl.when(array == 1)(partial(one, image_in))

        @pl.when(n == 0)
        def _():
            pl.semaphore_wait(barrier, len(peers))

        @pl.when(other == 1)
        def _():
            swap_copy(array, chunk).start()

        @pl.when(other == 0)
        def _():
            fan_out(array, chunk)

        return carry

    lax.fori_loop(0, 8, pack, 0)

    label_copy = remote(labels_in, labels, label_s, label_r, sibling)

    @pl.when(other == 0)
    def _():
        label_copy.start()
        labels[...] = labels_in[...]

    def relay_own(n, carry):
        array, chunk = n // 4, n % 4

        @pl.when(other == 1)
        def _():
            swap_wait(array, chunk)
            fan_out(array, chunk)

        @pl.when(n % 2 == 1)
        def _():
            for s in slots:
                pass_on(s, 0, n // 2)

        return carry

    lax.fori_loop(0, 8, relay_own, 0)

    @pl.when(other == 1)
    def _():
        label_copy.wait_recv()

    @pl.when(other == 0)
    def _():
        label_copy.wait_send()

    for b in range(4):
        row = labels[0:1, pl.ds(pl.multiple_of(512 * c + 128 * b, 128), 128)].astype(F32)
        label_column[0, 128 * b : 128 * b + 128, :] = jnp.broadcast_to(row, (128, 128)).T
    row = labels[0:1, :].astype(F32)
    place = lax.broadcasted_iota(jnp.int32, (8, 1024), 1).astype(F32)

    def invert(n, carry):
        base = (512 * c + 8 * n).astype(F32)
        this = lax.broadcasted_iota(jnp.int32, (8, 1024), 0).astype(F32) + base
        found = jnp.sum(jnp.where(row == this, place, 0.0), axis=1, keepdims=True)
        label_column[1, pl.ds(pl.multiple_of(8 * n, 8), 8), :] = jnp.broadcast_to(found, (8, 128))
        return carry

    lax.fori_loop(0, 64, invert, 0)

    def arrived(n, carry):
        core_copy(0, n // 4, n % 4, 1 - c).wait_recv()
        return carry

    lax.fori_loop(0, 8, arrived, 0)

    def own_rows(n, carry):
        array, part = n // 2, n % 2
        normalise(raw, 0, 1 - array, 2 * c + part, q.at[array], pl.multiple_of(part * CHUNK, CHUNK))
        return carry

    lax.fori_loop(0, 4, own_rows, 0)

    scale, bias = scalars[0], scalars[1]

    def gradient(array, carry):
        acc[...] = jnp.zeros_like(acc)

        def tile(m, inner):
            s, part = m % 4, m // 4
            ahead = 8 * array + m + 2
            for slot in slots:
                for p in range(2):

                    @pl.when(ahead == 8 + 4 * p + slot)
                    def _(slot=slot, p=p):
                        pass_on(slot, 1, 2 * p)
                        pass_on(slot, 1, 2 * p + 1)

            @pl.when(s > 0)
            def _():
                core_copy(s, array, 2 * part, 1 - c).wait_recv()
                core_copy(s, array, 2 * part + 1, 1 - c).wait_recv()

            for u in range(2):
                normalise(raw, s, array, 2 * part + u, kn, CHUNK * u)
            logits = lax.dot_general(q[array], kn[...], NT, preferred_element_type=F32) * scale + bias
            weight = jax.nn.sigmoid(logits)
            shift = (512 * part - 4096 * jnp.minimum(s, 1)).astype(F32)
            at = lax.broadcasted_iota(jnp.int32, (512, 128), 1).astype(F32) + shift
            column = label_column[array]
            positive = [jnp.where(column == at + 128.0 * u, 1.0, 0.0) for u in range(4)]
            weight = (weight - jnp.concatenate(positive, axis=1)).astype(BF)
            acc[...] += jnp.dot(weight, kn[...], preferred_element_type=F32)
            return inner

        lax.fori_loop(0, 8, tile, 0)

        for part in range(2):
            for r in range(0, HALF, 16):
                tails = []
                for side, (m0, m1, t) in enumerate(rows_of(raw, 0, 1 - array, 2 * c + part, r, low)):
                    rows = pl.ds(CHUNK * part + HALF * side + r, 16)
                    inverse = lax.rsqrt(lane_sum(m0 * m0, m1 * m1, t * t) + 1e-06)
                    m0, m1, t = m0 * inverse, m1 * inverse, t * inverse
                    g0, g1, gt = acc[rows, 0:512] * scale, acc[rows, 512:1024] * scale, acc[rows, 1024:1152] * scale
                    along = lane_sum(m0 * g0, m1 * g1, t * gt)
                    here = pl.ds(HALF * side + r, 16)
                    packed_out[array, 0, part, here, :] = (inverse * (g0 - m0 * along)).astype(BF)
                    packed_out[array, 1, part, here, :] = (inverse * (g1 - m1 * along)).astype(BF)
                    tails.append(inverse * (gt - t * along))
                for h, tail in enumerate(merge_tails(low, *tails)):
                    packed_out[array, h, part, tail_at(r)[0], tail_at(r)[1]] = tail.astype(BF)
        for part in range(2):
            last_copy(array, part, 1 - a, (me - c + a, 1 - a)).start()

            @pl.when(other == 1)
            def _(part=part):
                last_copy(array, part, a, sibling).start()

            @pl.when(other == 0)
            def _(part=part):
                home_copy(array, part).start()

        return carry

    def last_copy(array, part, half, device):
        return remote(
            packed_out.at[array, half, part], landed.at[array, 2 * c + part],
            last_s.at[array, half, part], last_r.at[array, 2 * c + part], device,
        )

    def home_copy(array, part):
        return pltpu.make_async_copy(
            packed_out.at[array, a, part], landed.at[array, 2 * c + part], last_r.at[array, 2 * c + part]
        )

    lax.fori_loop(0, 2, gradient, 0)

    for array, out in enumerate((image_out, text_out)):

        def unpack(chunk, carry, array=array, out=out):
            remote(
                packed_out.at[array, 0, 0], landed.at[array, chunk], last_s.at[array, 0, 0], last_r.at[array, chunk], across
            ).wait_recv()
            row = pl.multiple_of(chunk * CHUNK, CHUNK)
            out[pl.ds(row, CHUNK), 0:512] = landed[array, chunk, 0:CHUNK, :]
            for r in range(0, HALF, 16):
                pair = landed[array, chunk, tail_at(r)[0], tail_at(r)[1]].astype(F32)
                out[pl.ds(row + r, 16), 512:576] = pair[:, 0:64].astype(BF)
                out[pl.ds(row + HALF + r, 16), 512:576] = pltpu.roll(pair, 64, 1)[:, 0:64].astype(BF)
            return carry

        lax.fori_loop(0, 4, unpack, 0)

    def drain(n, carry):
        array, chunk = n // 4, n % 4

        @pl.when(other == 1)
        def _():
            swap_copy(array, chunk).wait_send()

        for s in direct:
            link_copy(s, array, chunk).wait_send()
        for s in relays:
            relay_copy(s, array, chunk).wait_send()
        for s in range(4):
            core_copy(s, array, chunk, c).wait_send()
        return carry

    lax.fori_loop(0, 8, drain, 0)
    for array in range(2):
        for part in range(2):
            last_copy(array, part, 1 - a, (me - c + a, 1 - a)).wait_send()

            @pl.when(other == 1)
            def _(array=array, part=part):
                last_copy(array, part, a, sibling).wait_send()


def call(bits, number, scalars, labels, text, image):
    dma = pltpu.SemaphoreType.DMA
    vmem = pl.BlockSpec(memory_space=pltpu.VMEM)
    return pl.pallas_call(
        partial(kernel, bits),
        out_shape=[jax.ShapeDtypeStruct(text.shape, BF)] * 2,
        in_specs=[pl.BlockSpec(memory_space=pltpu.SMEM)] + [vmem] * 3,
        out_specs=[vmem] * 2,
        scratch_shapes=[
            pltpu.VMEM((5, 2, 2, 4, PACKED, 512), BF),
            pltpu.VMEM((2, 512, 1152), BF),
            pltpu.VMEM((512, 1152), BF),
            pltpu.VMEM((512, 1152), F32),
            pltpu.VMEM((2, 2, 2, PACKED, 512), BF),
            pltpu.VMEM((2, 4, PACKED, 512), BF),
            pltpu.VMEM((1, 1024), jnp.int32),
            pltpu.VMEM((2, 512, 128), F32),
            dma((2, 4)), dma((2, 4)), dma((3, 2, 4)), dma((3, 2, 4)), dma((4, 2, 4)), dma((4, 2, 4)), dma((2, 4)),
            dma((2, 2, 2)), dma((2, 4)), dma, dma,
        ],
        compiler_params=pltpu.CompilerParams(
            collective_id=number, has_side_effects=True, vmem_limit_bytes=58 * 2**20
        ),
        cost_estimate=pl.CostEstimate(flops=20 * 10**9, bytes_accessed=6 * 10**6, transcendentals=4 * 2**20),
        name="rounds_" + "".join(map(str, bits)),
    )(scalars, labels, text, image)


def per_device(image, text, scale, bias, table, labels):
    choices = list(combinations(range(BITS), 3))
    mask = jnp.sum(table[:, 0])
    which = sum(jnp.where(mask == sum(1 << b for b in bits), n, 0) for n, bits in enumerate(choices))
    branches = [partial(call, bits, n) for n, bits in enumerate(choices)]
    scalars = jnp.stack([scale, bias])
    text_grad, image_grad = lax.switch(which.astype(jnp.int32), branches, scalars, labels, text, image)
    return image_grad.astype(F32), text_grad.astype(F32)


def solution(mesh):
    return jax.shard_map(
        per_device,
        mesh=mesh,
        in_specs=(P("dp", "tower"), P("dp", "tower"), P(), P(), P(), P("dp", None)),
        out_specs=(P("dp", "tower"), P("dp", "tower")),
        check_vma=False,
    )
```

```python
from functools import partial

import jax
import jax.numpy as jnp
from jax import lax
from jax.experimental import pallas as pl
from jax.experimental.pallas import tpu as pltpu
from jax.sharding import PartitionSpec as P

MESH = pl.DeviceIdType.MESH
BF = jnp.bfloat16
F32 = jnp.float32
NT = (((1,), (1,)), ((), ()))
WIDTH, DEPTH, ROWS = 1152, 576, 1024
CHUNK, TILE = 256, 512
SLOT_OF_BIT = (5, 1, 2, 6, 3, 4)
NEAR = (1, 3, 5)


def flip(index, bit):
    return index + (1 - 2 * ((index // (1 << bit)) % 2)) * (1 << bit)


def columns_of(half):
    return pl.ds(pl.multiple_of(DEPTH * half, DEPTH), DEPTH)


def rows_of(chunk):
    return pl.ds(CHUNK * chunk, CHUNK)


def kernel(
    table, scale_in, bias_in, labels_in, text_in, image_in, text_out, image_out,
    text_a, text_b, image_a, image_b, mine, q, kn, acc, gradient_out, labels, label_column,
    swap_s, swap_r, link_s, link_r, core_s, core_r, relay_s, last_s, last_r, label_s, label_r,
):
    me, a = lax.axis_index("dp"), lax.axis_index("tower")
    c = me % 2
    other = (c - a) * (c - a)
    sibling = (me + 1 - 2 * c, a)
    across = (me, 1 - a)
    diagonal = (me + 1 - 2 * c, 1 - a)
    home = (me - c + a, 1 - a)
    near = {1: (flip(me, 1), a), 3: (flip(me, 4), a), 5: across}
    beyond = {1: (flip(flip(me, 1), 2), a), 3: (flip(flip(me, 4), 5), a), 5: (flip(me, 3), 1 - a)}
    inputs, outputs = (text_in, image_in), (image_out, text_out)
    buffers = ((text_a, text_b), (image_a, image_b))

    barrier = pltpu.get_barrier_semaphore()
    peers = [sibling, across, diagonal, near[1], near[3], *beyond.values()]
    for peer in peers:
        pl.semaphore_signal(barrier, inc=1, device_id=peer, device_id_type=MESH)

    def remote(src, dst, send, recv, device):
        return pltpu.make_async_remote_copy(
            src_ref=src, dst_ref=dst, send_sem=send, recv_sem=recv, device_id=device, device_id_type=MESH
        )

    def place(slot, array, half, chunk):
        return buffers[array][chunk // 2].at[slot, columns_of(half), rows_of(chunk % 2)]

    def swap_copy(array, chunk):
        return remote(
            inputs[array].at[:, rows_of(chunk)], place(0, array, a, chunk),
            swap_s.at[array, chunk], swap_r.at[array, chunk], (me - c + a, c),
        )

    def swap_wait(array, chunk):
        remote(
            inputs[array].at[:, rows_of(chunk)], place(0, array, c, chunk),
            swap_s.at[array, chunk], swap_r.at[array, chunk], (me - c + a, c),
        ).wait_recv()

    def own_copy(array, chunk):
        return pltpu.make_async_copy(
            inputs[array].at[:, rows_of(chunk)], place(0, array, a, chunk), swap_r.at[array, chunk]
        )

    def beside_copy(array, chunk):
        return remote(
            inputs[array].at[:, rows_of(chunk)], place(5, array, a, chunk),
            link_s.at[2, array, chunk], link_r.at[4, array, chunk], sibling,
        )

    def link_copy(s, array, chunk):
        return remote(
            place(0, array, c, chunk), place(s, array, c, chunk),
            link_s.at[s // 2, array, chunk], link_r.at[s - 1, array, chunk], near[s],
        )

    def relay_copy(s, array, chunk):
        return remote(
            place(s, array, c, chunk), place(s + 1, array, c, chunk),
            relay_s.at[s // 2, array, chunk], link_r.at[s, array, chunk], beyond[s],
        )

    def core_copy(s, array, chunk, half):
        return remote(
            place(s, array, half, chunk), place(s, array, half, chunk),
            core_s.at[s, array, chunk], core_r.at[s, array, chunk], sibling,
        )

    def last_copy(array, half, device):
        return remote(
            gradient_out.at[array, columns_of(half), :],
            outputs[array].at[:, pl.ds(pl.multiple_of(TILE * c, TILE), TILE)],
            last_s.at[array, half], last_r.at[array, c], device,
        )

    def home_copy(array):
        return pltpu.make_async_copy(
            gradient_out.at[array, columns_of(a), :],
            outputs[array].at[:, pl.ds(pl.multiple_of(TILE * c, TILE), TILE)],
            last_r.at[array, c],
        )

    def pass_on(s, array, chunk):
        remote(
            place(0, array, c, chunk), place(s, array, c, chunk),
            link_s.at[0, array, chunk], link_r.at[s - 1, array, chunk], across,
        ).wait_recv()
        if s in NEAR:
            relay_copy(s, array, chunk).start()
        core_copy(s, array, chunk, c).start()

    def fan_out(array, chunk):
        link_copy(1, array, chunk).start()
        link_copy(3, array, chunk).start()
        core_copy(0, array, chunk, c).start()

    def pass_text(chunk):
        for s in (1, 3):
            pass_on(s, 0, chunk)
        if chunk > 0:
            for s in (2, 4):
                pass_on(s, 0, chunk - 1)

    chunks = [(array, chunk) for array in range(2) for chunk in range(4)]
    label_copy = remote(labels_in, labels, label_s, label_r, sibling)

    @pl.when(other == 0)
    def _():
        for which in chunks:
            own_copy(*which).start()

    pl.semaphore_wait(barrier, len(peers))

    @pl.when(other == 0)
    def _():
        for which in chunks:
            own_copy(*which).wait()
            fan_out(*which)
        label_copy.start()
        labels[...] = labels_in[...]
        for which in chunks:
            pass_on(5, *which)
        for chunk in range(4):
            pass_text(chunk)
        label_copy.wait_send()

    @pl.when(other == 1)
    def _():
        for which in chunks:
            swap_copy(*which).start()
        for which in chunks:
            beside_copy(*which).start()
        for n, which in enumerate(chunks):
            swap_wait(*which)
            fan_out(*which)
            if n > 0:
                pass_on(6, *chunks[n - 1])
            if n % 2 == 1:
                pass_text(n // 2)
        pass_on(6, *chunks[7])
        label_copy.wait_recv()

    for b in range(4):
        row = labels[0:1, pl.ds(pl.multiple_of(512 * c + 128 * b, 128), 128)].astype(F32)
        label_column[0, 128 * b : 128 * b + 128, :] = jnp.broadcast_to(row, (128, 128)).T
    row = labels[0:1, :].astype(F32)
    position = lax.broadcasted_iota(jnp.int32, (8, 1024), 1).astype(F32)

    def invert(n, carry):
        base = (512 * c + 8 * n).astype(F32)
        this = lax.broadcasted_iota(jnp.int32, (8, 1024), 0).astype(F32) + base
        found = jnp.sum(jnp.where(row == this, position, 0.0), axis=1, keepdims=True)
        label_column[1, pl.ds(pl.multiple_of(8 * n, 8), 8), :] = jnp.broadcast_to(found, (8, 128))
        return carry

    lax.fori_loop(0, 64, invert, 0)

    for which in chunks:
        core_copy(0, *which, 1 - c).wait_recv()

    @pl.when(other == 0)
    def _():
        for which in chunks:
            link_copy(5, *which).start()

    def inverse_norms(load):
        total = jnp.zeros((16, TILE), F32)
        for r in range(0, WIDTH, 16):
            part = load(r).astype(F32)
            total += part * part
        return lax.rsqrt(jnp.sum(total, axis=0, keepdims=True) + 1e-06)

    def normalise(load):
        inverse = inverse_norms(load)
        for r in range(0, WIDTH, 16):
            kn[r : r + 16, :] = (load(r).astype(F32) * inverse).astype(BF)

    for part in range(2):

        @pl.when(c == part)
        def _(part=part):
            mine[0] = text_a[0] if part == 0 else text_b[0]
            mine[1] = image_a[0] if part == 0 else image_b[0]

    def own_rows(array, carry):
        normalise(lambda r: mine[1 - array, r : r + 16, :])
        for b in range(0, WIDTH, 128):
            q[array, :, b : b + 128] = kn[b : b + 128, :].astype(F32).T.astype(BF)
        return carry

    lax.fori_loop(0, 2, own_rows, 0)
    acc[...] = jnp.zeros_like(acc)
    scale, bias = scale_in[0], bias_in[0]

    for_all = {
        2: [((2, 4), 0, 3)], 3: [((1, 3), 1, 0)], 4: [((2, 4), 1, 0)], 5: [((1, 3), 1, 1)], 7: [((2, 4), 1, 1), ((1, 3), 1, 2)],
        9: [((2, 4), 1, 2)], 10: [((1, 3), 1, 3)], 12: [((2, 4), 1, 3)],
    }
    z_near = {1: (0, 0), 3: (0, 1), 4: (0, 2), 5: (0, 3), 6: (1, 0), 7: (1, 1), 9: (1, 2), 10: (1, 3)}
    z_far = {3: (0, 0), 4: (0, 1), 5: (0, 2), 6: (0, 3), 8: (1, 0), 9: (1, 1), 11: (1, 2), 12: (1, 3)}

    def hand_over(step):
        for n in range(13):

            @pl.when(step == n)
            def _(n=n):
                if n in z_near:
                    pl.when(other == 1)(partial(pass_on, 5, *z_near[n]))
                if n in z_far:
                    pl.when(other == 0)(partial(pass_on, 6, *z_far[n]))
                for several, array, chunk in for_all.get(n, []):
                    for s in several:
                        pass_on(s, array, chunk)

    def finish(array):
        total = jnp.zeros((16, TILE), F32)
        for r in range(0, WIDTH, 16):
            total += mine[1 - array, r : r + 16, :].astype(F32) * acc[array, r : r + 16, :]
        inverse = inverse_norms(lambda r: mine[1 - array, r : r + 16, :])
        along = jnp.sum(total, axis=0, keepdims=True) * inverse * scale
        first, second = inverse * scale, inverse * inverse * along
        for r in range(0, WIDTH, 16):
            unit_part = mine[1 - array, r : r + 16, :].astype(F32) * second
            gradient_out[array, r : r + 16, :] = (first * acc[array, r : r + 16, :] - unit_part).astype(BF)

    def send(array):
        last_copy(array, 1 - a, home).start()

        @pl.when(other == 1)
        def _():
            last_copy(array, a, sibling).start()

        @pl.when(other == 0)
        def _():
            home_copy(array).start()

    def tile(step, carry):
        partnered = jnp.minimum(step // 4, 1)
        phase = (1 - partnered) * step + partnered * ((step - 4) // 3)
        array, part = phase // 2, phase % 2
        hand_over(step)
        value = table[(step + 2) % 3, 0]
        slot = sum(jnp.where(value == 1 << b, s, 0) for b, s in enumerate(SLOT_OF_BIT))
        for p in range(4):
            buffer = buffers[p // 2][p % 2]

            @pl.when(step == p)
            def _(buffer=buffer):
                normalise(lambda r: buffer[0, r : r + 16, :])

            @pl.when(step == 4 + 3 * p)
            def _(p=p):
                for s in range(1, 7):
                    for u in range(2):
                        core_copy(s, p // 2, 2 * (p % 2) + u, 1 - c).wait_recv()

            @pl.when((step >= 4 + 3 * p) & (step < 7 + 3 * p))
            def _(buffer=buffer):
                normalise(lambda r: buffer[slot, r : r + 16, :])

        logits = jnp.dot(q[array], kn[...], preferred_element_type=F32) * scale + bias
        weight = jax.nn.sigmoid(logits)
        shift = (TILE * part - 4096 * partnered).astype(F32)
        at = lax.broadcasted_iota(jnp.int32, (TILE, 128), 1).astype(F32) + shift
        column = label_column[array]
        positive = [jnp.where(column == at + 128.0 * u, 1.0, 0.0) for u in range(TILE // 128)]
        weight = (weight - jnp.concatenate(positive, axis=1)).astype(BF)
        acc[array] += lax.dot_general(kn[...], weight, NT, preferred_element_type=F32)

        @pl.when((step == 9) | (step == 15))
        def _():
            finish(array)

        pl.when(step == 9)(partial(send, 0))
        pl.when(step == 15)(partial(send, 1))
        return carry

    lax.fori_loop(0, 16, tile, 0)

    for array, chunk in chunks:
        for s in NEAR:
            link_copy(s, array, chunk).wait_send()
            relay_copy(s, array, chunk).wait_send()
        for s in range(7):
            core_copy(s, array, chunk, c).wait_send()

        @pl.when(other == 1)
        def _(array=array, chunk=chunk):
            swap_copy(array, chunk).wait_send()

    for array in range(2):
        for part in range(2):
            there = outputs[array].at[:, pl.ds(TILE * part, TILE)]
            here = (1 - other) * (1 - (part - c) * (part - c))

            @pl.when(here == 1)
            def _(array=array, part=part, there=there):
                pltpu.make_async_copy(gradient_out.at[array, columns_of(0), :], there, last_r.at[array, part]).wait()

            @pl.when(here == 0)
            def _(array=array, part=part, there=there):
                remote(
                    gradient_out.at[array, columns_of(0), :], there,
                    last_s.at[array, 0], last_r.at[array, part], across,
                ).wait_recv()

        last_copy(array, 1 - a, home).wait_send()

        @pl.when(other == 1)
        def _(array=array):
            last_copy(array, a, sibling).wait_send()


def per_device(image, text, scale, bias, table, labels):
    dma = pltpu.SemaphoreType.DMA
    smem, vmem = pl.BlockSpec(memory_space=pltpu.SMEM), pl.BlockSpec(memory_space=pltpu.VMEM)
    anywhere = pl.BlockSpec(memory_space=pl.ANY)
    text_grad, image_grad = pl.pallas_call(
        kernel,
        out_shape=[jax.ShapeDtypeStruct((DEPTH, ROWS), BF)] * 2,
        in_specs=[smem, smem, smem, vmem, anywhere, anywhere],
        out_specs=[anywhere] * 2,
        scratch_shapes=[pltpu.VMEM((7, WIDTH, TILE), BF)] * 4
        + [
            pltpu.VMEM((2, WIDTH, TILE), BF),
            pltpu.VMEM((2, TILE, WIDTH), BF),
            pltpu.VMEM((WIDTH, TILE), BF),
            pltpu.VMEM((2, WIDTH, TILE), F32),
            pltpu.VMEM((2, WIDTH, TILE), BF),
            pltpu.VMEM((1, ROWS), jnp.int32),
            pltpu.VMEM((2, TILE, 128), F32),
            dma((2, 4)), dma((2, 4)), dma((3, 2, 4)), dma((6, 2, 4)), dma((7, 2, 4)), dma((7, 2, 4)), dma((3, 2, 4)),
            dma((2, 2)), dma((2, 2)), dma, dma,
        ],
        compiler_params=pltpu.CompilerParams(collective_id=0, has_side_effects=True, vmem_limit_bytes=58 * 2**20),
        cost_estimate=pl.CostEstimate(flops=20 * 10**9, bytes_accessed=6 * 10**6, transcendentals=4 * 2**20),
        name="rounds",
    )(table, scale.reshape(1), bias.reshape(1), labels, text.T, image.T)
    return image_grad.T.astype(F32), text_grad.T.astype(F32)


def solution(mesh):
    return jax.shard_map(
        per_device,
        mesh=mesh,
        in_specs=(P("dp", "tower"), P("dp", "tower"), P(), P(), P(), P("dp", None)),
        out_specs=(P("dp", "tower"), P("dp", "tower")),
        check_vma=False,
    )
```

```python
from functools import partial

import jax
import jax.numpy as jnp
from jax import lax
from jax.experimental import pallas as pl
from jax.experimental.pallas import tpu as pltpu
from jax.sharding import PartitionSpec as P

MESH = pl.DeviceIdType.MESH
BF = jnp.bfloat16
F32 = jnp.float32
NT = (((1,), (1,)), ((), ()))
WIDTH, DEPTH, ROWS = 1152, 576, 1024
CHUNK, TILE = 256, 512
SLOT_OF_BIT = (5, 1, 2, 6, 3, 4)
NEAR = (1, 3, 5)
GATE = 5


def flip(index, bit):
    return index + (1 - 2 * ((index // (1 << bit)) % 2)) * (1 << bit)


def columns_of(half):
    return pl.ds(pl.multiple_of(DEPTH * half, DEPTH), DEPTH)


def rows_of(chunk):
    return pl.ds(CHUNK * chunk, CHUNK)


def kernel(
    table, scale_in, bias_in, labels_in, text_in, image_in, text_out, image_out,
    text_a, text_b, image_a, image_b, mine, q, kn, acc, gradient_out, labels, label_column,
    swap_s, swap_r, link_s, link_r, core_s, core_r, relay_s, last_s, last_r, label_s, label_r,
):
    me, a = lax.axis_index("dp"), lax.axis_index("tower")
    c = me % 2
    other = (c - a) * (c - a)
    sibling = (me + 1 - 2 * c, a)
    across = (me, 1 - a)
    diagonal = (me + 1 - 2 * c, 1 - a)
    home = (me - c + a, 1 - a)
    near = {1: (flip(me, 1), a), 3: (flip(me, 4), a), 5: across}
    beyond = {1: (flip(flip(me, 1), 2), a), 3: (flip(flip(me, 4), 5), a), 5: (flip(me, 3), 1 - a)}
    inputs, outputs = (text_in, image_in), (image_out, text_out)
    buffers = ((text_a, text_b), (image_a, image_b))

    barrier = pltpu.get_barrier_semaphore()
    peers = [sibling, across, diagonal, near[1], near[3], *beyond.values()]
    for peer in peers:
        pl.semaphore_signal(barrier, inc=1, device_id=peer, device_id_type=MESH)

    def remote(src, dst, send, recv, device):
        return pltpu.make_async_remote_copy(
            src_ref=src, dst_ref=dst, send_sem=send, recv_sem=recv, device_id=device, device_id_type=MESH
        )

    def place(slot, array, half, chunk):
        return buffers[array][chunk // 2].at[slot, columns_of(half), rows_of(chunk % 2)]

    def swap_copy(array, chunk):
        return remote(
            inputs[array].at[:, rows_of(chunk)], place(0, array, a, chunk),
            swap_s.at[array, chunk], swap_r.at[array, chunk], (me - c + a, c),
        )

    def swap_wait(array, chunk):
        remote(
            inputs[array].at[:, rows_of(chunk)], place(0, array, c, chunk),
            swap_s.at[array, chunk], swap_r.at[array, chunk], (me - c + a, c),
        ).wait_recv()

    def own_copy(array, chunk):
        return pltpu.make_async_copy(
            inputs[array].at[:, rows_of(chunk)], place(0, array, a, chunk), swap_r.at[array, chunk]
        )

    def beside_copy(array, chunk):
        return remote(
            inputs[array].at[:, rows_of(chunk)], place(5, array, a, chunk),
            link_s.at[2, array, chunk], link_r.at[4, array, chunk], sibling,
        )

    def link_copy(s, array, chunk):
        return remote(
            place(0, array, c, chunk), place(s, array, c, chunk),
            link_s.at[s // 2, array, chunk], link_r.at[s - 1, array, chunk], near[s],
        )

    def relay_copy(s, array, chunk):
        return remote(
            place(s, array, c, chunk), place(s + 1, array, c, chunk),
            relay_s.at[s // 2, array, chunk], link_r.at[s, array, chunk], beyond[s],
        )

    def core_copy(s, array, chunk, half):
        return remote(
            place(s, array, half, chunk), place(s, array, half, chunk),
            core_s.at[s, array, chunk], core_r.at[s, array, chunk], sibling,
        )

    def last_copy(array, half, device):
        return remote(
            gradient_out.at[array, columns_of(half), :],
            outputs[array].at[:, pl.ds(pl.multiple_of(TILE * c, TILE), TILE)],
            last_s.at[array, half], last_r.at[array, c], device,
        )

    def home_copy(array):
        return pltpu.make_async_copy(
            gradient_out.at[array, columns_of(a), :],
            outputs[array].at[:, pl.ds(pl.multiple_of(TILE * c, TILE), TILE)],
            last_r.at[array, c],
        )

    def pass_on(s, array, chunk):
        remote(
            place(0, array, c, chunk), place(s, array, c, chunk),
            link_s.at[0, array, chunk], link_r.at[s - 1, array, chunk], across,
        ).wait_recv()
        if s in NEAR:
            relay_copy(s, array, chunk).start()
        core_copy(s, array, chunk, c).start()

    def fan_out(array, chunk):
        link_copy(1, array, chunk).start()
        link_copy(3, array, chunk).start()
        core_copy(0, array, chunk, c).start()

    def pass_text(chunk):
        for s in (1, 3):
            pass_on(s, 0, chunk)
        if chunk > 1:
            for s in (2, 4):
                pass_on(s, 0, chunk - 2)

    chunks = [(array, chunk) for array in range(2) for chunk in range(4)]
    label_copy = remote(labels_in, labels, label_s, label_r, sibling)

    @pl.when(other == 0)
    def _():
        for which in chunks:
            own_copy(*which).start()

    pl.semaphore_wait(barrier, len(peers))

    @pl.when(other == 0)
    def _():
        label_copy.start()
        labels[...] = labels_in[...]
        for which in chunks:
            own_copy(*which).wait()
            fan_out(*which)
        label_copy.wait_send()

    @pl.when(other == 1)
    def _():
        for which in chunks:
            swap_copy(*which).start()
        for which in chunks:
            beside_copy(*which).start()
        label_copy.wait_recv()

    for b in range(4):
        row = labels[0:1, pl.ds(pl.multiple_of(512 * c + 128 * b, 128), 128)].astype(F32)
        label_column[0, 128 * b : 128 * b + 128, :] = jnp.broadcast_to(row, (128, 128)).T
    row = labels[0:1, :].astype(F32)
    position = lax.broadcasted_iota(jnp.int32, (8, 1024), 1).astype(F32)

    def invert(n, carry):
        base = (512 * c + 8 * n).astype(F32)
        this = lax.broadcasted_iota(jnp.int32, (8, 1024), 0).astype(F32) + base
        found = jnp.sum(jnp.where(row == this, position, 0.0), axis=1, keepdims=True)
        label_column[1, pl.ds(pl.multiple_of(8 * n, 8), 8), :] = jnp.broadcast_to(found, (8, 128))
        return carry

    lax.fori_loop(0, 64, invert, 0)

    def swapped_in(first, last):
        for n in range(first, last):
            swap_wait(*chunks[n])
            fan_out(*chunks[n])
            if n > 1:
                pass_on(6, *chunks[n - 2])
            if n % 2 == 1:
                pass_text(n // 2)

    @pl.when(other == 0)
    def _():
        for which in chunks:
            pass_on(5, *which)
        pass_text(0)
        pass_text(1)

    pl.when(other == 1)(partial(swapped_in, 0, 5))

    def inverse_norms(load):
        total = jnp.zeros((16, TILE), F32)
        for r in range(0, WIDTH, 16):
            part = load(r).astype(F32)
            total += part * part
        return lax.rsqrt(jnp.sum(total, axis=0, keepdims=True) + 1e-06)

    def normalise(load):
        inverse = inverse_norms(load)
        for r in range(0, WIDTH, 16):
            kn[r : r + 16, :] = (load(r).astype(F32) * inverse).astype(BF)

    def own_rows(array):
        for part in range(2):

            @pl.when(c == part)
            def _(part=part):
                mine[array] = buffers[array][part][0]

        normalise(lambda r: mine[array, r : r + 16, :])
        for b in range(0, WIDTH, 128):
            q[1 - array, :, b : b + 128] = kn[b : b + 128, :].astype(F32).T.astype(BF)

    for chunk in range(4):
        core_copy(0, 0, chunk, 1 - c).wait_recv()
    own_rows(0)

    @pl.when(other == 0)
    def _():
        pass_text(2)
        for n in range(4, 8):
            if n <= GATE:
                core_copy(0, *chunks[n], 1 - c).wait_recv()
        for first in chunks[: 7 - GATE]:
            link_copy(5, *first).start()
        for n in range(GATE + 1, 8):
            core_copy(0, *chunks[n], 1 - c).wait_recv()
        for which in chunks[7 - GATE :]:
            link_copy(5, *which).start()
        pass_text(3)

    @pl.when(other == 1)
    def _():
        swapped_in(5, 8)
        pass_on(6, *chunks[6])
        pass_on(6, *chunks[7])
        for n in range(4, 8):
            core_copy(0, *chunks[n], 1 - c).wait_recv()

    own_rows(1)
    acc[...] = jnp.zeros_like(acc)
    scale, bias = scale_in[0], bias_in[0]

    plan = {
        0: [((2, 4), 0, 2)],
        1: [((5,), 0, 0)],
        2: [((1, 3), 1, 0)],
        3: [((5,), 0, 1), ((2, 4), 0, 3), ((6,), 0, 0)],
        4: [((5,), 0, 2), ((6,), 0, 1), ((1, 3), 1, 1), ((5,), 0, 3)],
        5: [((2, 4), 1, 0), ((6,), 0, 2)],
        6: [((5,), 1, 0)],
        7: [((6,), 0, 3), ((1, 3), 1, 2)],
        8: [((5,), 1, 1), ((2, 4), 1, 1), ((6,), 1, 0)],
        9: [((5,), 1, 2)],
        10: [((6,), 1, 1), ((1, 3), 1, 3), ((5,), 1, 3)],
        11: [((2, 4), 1, 2), ((6,), 1, 2)],
        13: [((6,), 1, 3), ((2, 4), 1, 3)],
    }

    def hand_over(n):
        for several, array, chunk in plan.get(n, []):
            for s in several:
                if s == 5:
                    pl.when(other == 1)(partial(pass_on, s, array, chunk))
                elif s == 6:
                    pl.when(other == 0)(partial(pass_on, s, array, chunk))
                else:
                    pass_on(s, array, chunk)

    def finish(array):
        total = jnp.zeros((16, TILE), F32)
        for r in range(0, WIDTH, 16):
            total += mine[1 - array, r : r + 16, :].astype(F32) * acc[array, r : r + 16, :]
        inverse = inverse_norms(lambda r: mine[1 - array, r : r + 16, :])
        along = jnp.sum(total, axis=0, keepdims=True) * inverse * scale
        first, second = inverse * scale, inverse * inverse * along
        for r in range(0, WIDTH, 16):
            unit_part = mine[1 - array, r : r + 16, :].astype(F32) * second
            gradient_out[array, r : r + 16, :] = (first * acc[array, r : r + 16, :] - unit_part).astype(BF)

    def send(array):
        last_copy(array, 1 - a, home).start()

        @pl.when(other == 1)
        def _():
            last_copy(array, a, sibling).start()

        @pl.when(other == 0)
        def _():
            home_copy(array).start()

    def tile(load, array, part, own):
        normalise(load)
        logits = jnp.dot(q[array], kn[...], preferred_element_type=F32) * scale + bias
        weight = jax.nn.sigmoid(logits)
        if own:
            at = lax.broadcasted_iota(jnp.int32, (TILE, 128), 1).astype(F32) + float(TILE * part)
            column = label_column[array]
            positive = [jnp.where(column == at + 128.0 * u, 1.0, 0.0) for u in range(TILE // 128)]
            weight = weight - jnp.concatenate(positive, axis=1)
        acc[array] += lax.dot_general(kn[...], weight.astype(BF), NT, preferred_element_type=F32)

    for n in range(4):
        array, part = n // 2, n % 2
        hand_over(n)
        tile(lambda r, buffer=buffers[array][part]: buffer[0, r : r + 16, :], array, part, True)

    for n in range(4):
        array, part = n // 2, n % 2
        buffer = buffers[array][part]
        hand_over(4 + 3 * n)
        for s in range(1, 7):
            for u in range(2):
                core_copy(s, array, 2 * part + u, 1 - c).wait_recv()

        def partner_tile(k, carry, n=n, array=array, part=part, buffer=buffer):
            for later in (1, 2):
                pl.when(k == later)(partial(hand_over, 4 + 3 * n + later))
            value = table[k, 0]
            slot = sum(jnp.where(value == 1 << b, s, 0) for b, s in enumerate(SLOT_OF_BIT))
            tile(lambda r: buffer[slot, r : r + 16, :], array, part, False)
            return carry

        lax.fori_loop(0, 3, partner_tile, 0)
        if part == 1:
            finish(array)
            send(array)

    for array, chunk in chunks:
        for s in NEAR:
            link_copy(s, array, chunk).wait_send()
            relay_copy(s, array, chunk).wait_send()
        for s in range(7):
            core_copy(s, array, chunk, c).wait_send()

        @pl.when(other == 1)
        def _(array=array, chunk=chunk):
            swap_copy(array, chunk).wait_send()

    for array in range(2):
        for part in range(2):
            there = outputs[array].at[:, pl.ds(TILE * part, TILE)]
            here = (1 - other) * (1 - (part - c) * (part - c))

            @pl.when(here == 1)
            def _(array=array, part=part, there=there):
                pltpu.make_async_copy(gradient_out.at[array, columns_of(0), :], there, last_r.at[array, part]).wait()

            @pl.when(here == 0)
            def _(array=array, part=part, there=there):
                remote(
                    gradient_out.at[array, columns_of(0), :], there,
                    last_s.at[array, 0], last_r.at[array, part], across,
                ).wait_recv()

        last_copy(array, 1 - a, home).wait_send()

        @pl.when(other == 1)
        def _(array=array):
            last_copy(array, a, sibling).wait_send()


def per_device(image, text, scale, bias, table, labels):
    dma = pltpu.SemaphoreType.DMA
    smem, vmem = pl.BlockSpec(memory_space=pltpu.SMEM), pl.BlockSpec(memory_space=pltpu.VMEM)
    anywhere = pl.BlockSpec(memory_space=pl.ANY)
    text_grad, image_grad = pl.pallas_call(
        kernel,
        out_shape=[jax.ShapeDtypeStruct((DEPTH, ROWS), BF)] * 2,
        in_specs=[smem, smem, smem, vmem, anywhere, anywhere],
        out_specs=[anywhere] * 2,
        scratch_shapes=[pltpu.VMEM((7, WIDTH, TILE), BF)] * 4
        + [
            pltpu.VMEM((2, WIDTH, TILE), BF),
            pltpu.VMEM((2, TILE, WIDTH), BF),
            pltpu.VMEM((WIDTH, TILE), BF),
            pltpu.VMEM((2, WIDTH, TILE), F32),
            pltpu.VMEM((2, WIDTH, TILE), BF),
            pltpu.VMEM((1, ROWS), jnp.int32),
            pltpu.VMEM((2, TILE, 128), F32),
            dma((2, 4)), dma((2, 4)), dma((3, 2, 4)), dma((6, 2, 4)), dma((7, 2, 4)), dma((7, 2, 4)), dma((3, 2, 4)),
            dma((2, 2)), dma((2, 2)), dma, dma,
        ],
        compiler_params=pltpu.CompilerParams(collective_id=0, has_side_effects=True, vmem_limit_bytes=58 * 2**20),
        cost_estimate=pl.CostEstimate(flops=20 * 10**9, bytes_accessed=6 * 10**6, transcendentals=4 * 2**20),
        name="rounds",
    )(table, scale.reshape(1), bias.reshape(1), labels, text.T, image.T)
    return image_grad.T.astype(F32), text_grad.T.astype(F32)


def solution(mesh):
    return jax.shard_map(
        per_device,
        mesh=mesh,
        in_specs=(P("dp", "tower"), P("dp", "tower"), P(), P(), P(), P("dp", None)),
        out_specs=(P("dp", "tower"), P("dp", "tower")),
        check_vma=False,
    )
```

```python
from functools import partial

import jax
import jax.numpy as jnp
from jax import lax
from jax.experimental import pallas as pl
from jax.experimental.pallas import tpu as pltpu
from jax.sharding import PartitionSpec as P

MESH = pl.DeviceIdType.MESH
BF = jnp.bfloat16
F32 = jnp.float32
NT = (((1,), (1,)), ((), ()))
WIDTH, DEPTH, ROWS = 1152, 576, 1024
CHUNK, TILE = 256, 512
SLOT_OF_BIT = (5, 1, 2, 6, 3, 4)
NEAR = (1, 3, 5)
GATE = 5


def flip(index, bit):
    return index + (1 - 2 * ((index // (1 << bit)) % 2)) * (1 << bit)


def columns_of(half):
    return pl.ds(pl.multiple_of(DEPTH * half, DEPTH), DEPTH)


def rows_of(chunk):
    return pl.ds(CHUNK * chunk, CHUNK)


def kernel(
    table, scale_in, bias_in, labels_in, text_in, image_in, text_out, image_out,
    text_a, text_b, image_a, image_b, mine, q, kn, acc, gradient_out, labels, label_column,
    swap_s, swap_r, link_s, link_r, core_s, core_r, relay_s, last_s, last_r, label_s, label_r,
):
    me, a = lax.axis_index("dp"), lax.axis_index("tower")
    c = me % 2
    other = (c - a) * (c - a)
    sibling = (me + 1 - 2 * c, a)
    across = (me, 1 - a)
    diagonal = (me + 1 - 2 * c, 1 - a)
    home = (me - c + a, 1 - a)
    near = {1: (flip(me, 1), a), 3: (flip(me, 4), a), 5: across}
    beyond = {1: (flip(flip(me, 1), 2), a), 3: (flip(flip(me, 4), 5), a), 5: (flip(me, 3), 1 - a)}
    inputs, outputs = (text_in, image_in), (image_out, text_out)
    buffers = ((text_a, text_b), (image_a, image_b))

    barrier = pltpu.get_barrier_semaphore()
    peers = [sibling, across, diagonal, near[1], near[3], *beyond.values()]
    for peer in peers:
        pl.semaphore_signal(barrier, inc=1, device_id=peer, device_id_type=MESH)

    def remote(src, dst, send, recv, device):
        return pltpu.make_async_remote_copy(
            src_ref=src, dst_ref=dst, send_sem=send, recv_sem=recv, device_id=device, device_id_type=MESH
        )

    def place(slot, array, half, chunk):
        return buffers[array][chunk // 2].at[slot, columns_of(half), rows_of(chunk % 2)]

    def swap_copy(array, chunk):
        return remote(
            inputs[array].at[:, rows_of(chunk)], place(0, array, a, chunk),
            swap_s.at[array, chunk], swap_r.at[array, chunk], (me - c + a, c),
        )

    def swap_wait(array, chunk):
        remote(
            inputs[array].at[:, rows_of(chunk)], place(0, array, c, chunk),
            swap_s.at[array, chunk], swap_r.at[array, chunk], (me - c + a, c),
        ).wait_recv()

    def own_copy(array, chunk):
        return pltpu.make_async_copy(
            inputs[array].at[:, rows_of(chunk)], place(0, array, a, chunk), swap_r.at[array, chunk]
        )

    def beside_copy(array, chunk):
        return remote(
            inputs[array].at[:, rows_of(chunk)], place(5, array, a, chunk),
            link_s.at[2, array, chunk], link_r.at[4, array, chunk], sibling,
        )

    def link_copy(s, array, chunk):
        return remote(
            place(0, array, c, chunk), place(s, array, c, chunk),
            link_s.at[s // 2, array, chunk], link_r.at[s - 1, array, chunk], near[s],
        )

    def relay_copy(s, array, chunk):
        return remote(
            place(s, array, c, chunk), place(s + 1, array, c, chunk),
            relay_s.at[s // 2, array, chunk], link_r.at[s, array, chunk], beyond[s],
        )

    def core_copy(s, array, chunk, half):
        return remote(
            place(s, array, half, chunk), place(s, array, half, chunk),
            core_s.at[s, array, chunk], core_r.at[s, array, chunk], sibling,
        )

    def result(array, half, piece):
        return gradient_out.at[array, columns_of(half), rows_of(piece)]

    def landing(array, piece):
        row = pl.multiple_of(TILE * c + CHUNK * piece, CHUNK)
        return outputs[array].at[:, pl.ds(row, CHUNK)]

    def last_copy(array, half, piece, device):
        return remote(
            result(array, half, piece), landing(array, piece),
            last_s.at[array, half, piece], last_r.at[array, c, piece], device,
        )

    def home_copy(array, piece):
        return pltpu.make_async_copy(result(array, a, piece), landing(array, piece), last_r.at[array, c, piece])

    def pass_on(s, array, chunk):
        remote(
            place(0, array, c, chunk), place(s, array, c, chunk),
            link_s.at[0, array, chunk], link_r.at[s - 1, array, chunk], across,
        ).wait_recv()
        if s in NEAR:
            relay_copy(s, array, chunk).start()
        core_copy(s, array, chunk, c).start()

    def fan_out(array, chunk):
        link_copy(1, array, chunk).start()
        link_copy(3, array, chunk).start()
        core_copy(0, array, chunk, c).start()

    def pass_text(chunk):
        for s in (1, 3):
            pass_on(s, 0, chunk)
        if chunk > 1:
            for s in (2, 4):
                pass_on(s, 0, chunk - 2)

    chunks = [(array, chunk) for array in range(2) for chunk in range(4)]
    label_copy = remote(labels_in, labels, label_s, label_r, sibling)

    @pl.when(other == 0)
    def _():
        for which in chunks:
            own_copy(*which).start()

    pl.semaphore_wait(barrier, len(peers))

    @pl.when(other == 0)
    def _():
        label_copy.start()
        labels[...] = labels_in[...]
        for which in chunks:
            own_copy(*which).wait()
            fan_out(*which)
        label_copy.wait_send()

    @pl.when(other == 1)
    def _():
        for which in chunks:
            swap_copy(*which).start()
        for which in chunks:
            beside_copy(*which).start()
        label_copy.wait_recv()

    for b in range(4):
        row = labels[0:1, pl.ds(pl.multiple_of(512 * c + 128 * b, 128), 128)].astype(F32)
        label_column[0, 128 * b : 128 * b + 128, :] = jnp.broadcast_to(row, (128, 128)).T
    row = labels[0:1, :].astype(F32)
    position = lax.broadcasted_iota(jnp.int32, (8, 1024), 1).astype(F32)

    def invert(n, carry):
        base = (512 * c + 8 * n).astype(F32)
        this = lax.broadcasted_iota(jnp.int32, (8, 1024), 0).astype(F32) + base
        found = jnp.sum(jnp.where(row == this, position, 0.0), axis=1, keepdims=True)
        label_column[1, pl.ds(pl.multiple_of(8 * n, 8), 8), :] = jnp.broadcast_to(found, (8, 128))
        return carry

    lax.fori_loop(0, 64, invert, 0)

    def swapped_in(first, last):
        for n in range(first, last):
            swap_wait(*chunks[n])
            fan_out(*chunks[n])
            if n > 1:
                pass_on(6, *chunks[n - 2])
            if n % 2 == 1:
                pass_text(n // 2)

    @pl.when(other == 0)
    def _():
        for which in chunks:
            pass_on(5, *which)
        pass_text(0)
        pass_text(1)

    pl.when(other == 1)(partial(swapped_in, 0, 5))

    def inverse_norms(load):
        total = jnp.zeros((16, TILE), F32)
        for r in range(0, WIDTH, 16):
            part = load(r).astype(F32)
            total += part * part
        return lax.rsqrt(jnp.sum(total, axis=0, keepdims=True) + 1e-06)

    def normalise(load, k=0):
        inverse = inverse_norms(load)
        for r in range(0, WIDTH, 16):
            kn[k, r : r + 16, :] = (load(r).astype(F32) * inverse).astype(BF)

    def own_rows(array):
        for part in range(2):

            @pl.when(c == part)
            def _(part=part):
                mine[array] = buffers[array][part][0]

        normalise(lambda r: mine[array, r : r + 16, :])
        for b in range(0, WIDTH, 128):
            q[1 - array, :, b : b + 128] = kn[0, b : b + 128, :].astype(F32).T.astype(BF)

    for chunk in range(4):
        core_copy(0, 0, chunk, 1 - c).wait_recv()
    own_rows(0)

    @pl.when(other == 0)
    def _():
        pass_text(2)
        for n in range(4, 8):
            if n <= GATE:
                core_copy(0, *chunks[n], 1 - c).wait_recv()
        for first in chunks[: 7 - GATE]:
            link_copy(5, *first).start()
        for n in range(GATE + 1, 8):
            core_copy(0, *chunks[n], 1 - c).wait_recv()
        for which in chunks[7 - GATE :]:
            link_copy(5, *which).start()
        pass_text(3)

    @pl.when(other == 1)
    def _():
        swapped_in(5, 8)
        pass_on(6, *chunks[6])
        pass_on(6, *chunks[7])
        for n in range(4, 8):
            core_copy(0, *chunks[n], 1 - c).wait_recv()

    own_rows(1)
    acc[...] = jnp.zeros_like(acc)
    scale, bias = scale_in[0], bias_in[0]

    plan = {
        0: [((2, 4), 0, 2)],
        1: [((5,), 0, 0)],
        2: [((1, 3), 1, 0)],
        3: [((5,), 0, 1), ((2, 4), 0, 3), ((6,), 0, 0)],
        4: [((5,), 0, 2), ((6,), 0, 1), ((1, 3), 1, 1), ((5,), 0, 3)],
        5: [((2, 4), 1, 0), ((6,), 0, 2)],
        6: [((5,), 1, 0)],
        7: [((6,), 0, 3), ((1, 3), 1, 2)],
        8: [((5,), 1, 1), ((2, 4), 1, 1), ((6,), 1, 0)],
        9: [((5,), 1, 2)],
        10: [((6,), 1, 1), ((1, 3), 1, 3), ((5,), 1, 3)],
        11: [((2, 4), 1, 2), ((6,), 1, 2)],
        13: [((6,), 1, 3), ((2, 4), 1, 3)],
    }

    def hand_over(n):
        for several, array, chunk in plan.get(n, []):
            for s in several:
                if s == 5:
                    pl.when(other == 1)(partial(pass_on, s, array, chunk))
                elif s == 6:
                    pl.when(other == 0)(partial(pass_on, s, array, chunk))
                else:
                    pass_on(s, array, chunk)

    def finish(array, piece):
        rows = rows_of(piece)
        total = jnp.zeros((16, CHUNK), F32)
        square = jnp.zeros((16, CHUNK), F32)
        for r in range(0, WIDTH, 16):
            own = mine[1 - array, r : r + 16, rows].astype(F32)
            square += own * own
            total += own * acc[array, r : r + 16, rows]
        inverse = lax.rsqrt(jnp.sum(square, axis=0, keepdims=True) + 1e-06)
        along = jnp.sum(total, axis=0, keepdims=True) * inverse * scale
        first, second = inverse * scale, inverse * inverse * along
        for r in range(0, WIDTH, 16):
            unit_part = mine[1 - array, r : r + 16, rows].astype(F32) * second
            gradient_out[array, r : r + 16, rows] = (first * acc[array, r : r + 16, rows] - unit_part).astype(BF)
        last_copy(array, 1 - a, piece, home).start()

        @pl.when(other == 1)
        def _():
            last_copy(array, a, piece, sibling).start()

        @pl.when(other == 0)
        def _():
            home_copy(array, piece).start()

    def tile(array, part, own, k=0, first=0, size=TILE):
        rows = pl.ds(first, size)
        logits = jnp.dot(q[array, rows, :], kn[k], preferred_element_type=F32) * scale + bias
        weight = jax.nn.sigmoid(logits)
        if own:
            at = lax.broadcasted_iota(jnp.int32, (TILE, 128), 1).astype(F32) + float(TILE * part)
            column = label_column[array]
            positive = [jnp.where(column == at + 128.0 * u, 1.0, 0.0) for u in range(TILE // 128)]
            weight = weight - jnp.concatenate(positive, axis=1)
        acc[array, :, rows] += lax.dot_general(kn[k], weight.astype(BF), NT, preferred_element_type=F32)

    def slot_of(k):
        value = table[k, 0]
        return sum(jnp.where(value == 1 << b, s, 0) for b, s in enumerate(SLOT_OF_BIT))

    for n in range(4):
        array, part = n // 2, n % 2
        hand_over(n)
        normalise(lambda r, buffer=buffers[array][part]: buffer[0, r : r + 16, :])
        tile(array, part, True)

    for n in range(4):
        array, part = n // 2, n % 2
        buffer = buffers[array][part]
        hand_over(4 + 3 * n)
        for s in range(1, 7):
            for u in range(2):
                core_copy(s, array, 2 * part + u, 1 - c).wait_recv()

        if n == 3:
            for k in range(3):
                slot = slot_of(k)
                normalise(lambda r, slot=slot, buffer=buffer: buffer[slot, r : r + 16, :], k)
                tile(array, part, False, k, 0, CHUNK)
            finish(array, 0)
            for k in range(3):
                tile(array, part, False, k, CHUNK, CHUNK)
            finish(array, 1)
            continue

        def partner_tile(k, carry, n=n, array=array, part=part, buffer=buffer):
            for later in (1, 2):
                pl.when(k == later)(partial(hand_over, 4 + 3 * n + later))
            slot = slot_of(k)
            normalise(lambda r: buffer[slot, r : r + 16, :])
            tile(array, part, False)
            return carry

        lax.fori_loop(0, 3, partner_tile, 0)
        if n == 1:
            finish(array, 0)
            finish(array, 1)

    for array, chunk in chunks:
        for s in NEAR:
            link_copy(s, array, chunk).wait_send()
            relay_copy(s, array, chunk).wait_send()
        for s in range(7):
            core_copy(s, array, chunk, c).wait_send()

        @pl.when(other == 1)
        def _(array=array, chunk=chunk):
            swap_copy(array, chunk).wait_send()

    for array in range(2):
        for piece in range(2):
            for part in range(2):
                there = outputs[array].at[:, rows_of(2 * part + piece)]
                here = (1 - other) * (1 - (part - c) * (part - c))

                @pl.when(here == 1)
                def _(array=array, part=part, piece=piece, there=there):
                    pltpu.make_async_copy(result(array, 0, piece), there, last_r.at[array, part, piece]).wait()

                @pl.when(here == 0)
                def _(array=array, part=part, piece=piece, there=there):
                    remote(
                        result(array, 0, piece), there, last_s.at[array, 0, piece], last_r.at[array, part, piece], across
                    ).wait_recv()

            last_copy(array, 1 - a, piece, home).wait_send()

            @pl.when(other == 1)
            def _(array=array, piece=piece):
                last_copy(array, a, piece, sibling).wait_send()


def per_device(image, text, scale, bias, table, labels):
    dma = pltpu.SemaphoreType.DMA
    smem, vmem = pl.BlockSpec(memory_space=pltpu.SMEM), pl.BlockSpec(memory_space=pltpu.VMEM)
    anywhere = pl.BlockSpec(memory_space=pl.ANY)
    text_grad, image_grad = pl.pallas_call(
        kernel,
        out_shape=[jax.ShapeDtypeStruct((DEPTH, ROWS), BF)] * 2,
        in_specs=[smem, smem, smem, vmem, anywhere, anywhere],
        out_specs=[anywhere] * 2,
        scratch_shapes=[pltpu.VMEM((7, WIDTH, TILE), BF)] * 4
        + [
            pltpu.VMEM((2, WIDTH, TILE), BF),
            pltpu.VMEM((2, TILE, WIDTH), BF),
            pltpu.VMEM((3, WIDTH, TILE), BF),
            pltpu.VMEM((2, WIDTH, TILE), F32),
            pltpu.VMEM((2, WIDTH, TILE), BF),
            pltpu.VMEM((1, ROWS), jnp.int32),
            pltpu.VMEM((2, TILE, 128), F32),
            dma((2, 4)), dma((2, 4)), dma((3, 2, 4)), dma((6, 2, 4)), dma((7, 2, 4)), dma((7, 2, 4)), dma((3, 2, 4)),
            dma((2, 2, 2)), dma((2, 2, 2)), dma, dma,
        ],
        compiler_params=pltpu.CompilerParams(collective_id=0, has_side_effects=True, vmem_limit_bytes=58 * 2**20),
        cost_estimate=pl.CostEstimate(flops=20 * 10**9, bytes_accessed=6 * 10**6, transcendentals=4 * 2**20),
        name="rounds",
    )(table, scale.reshape(1), bias.reshape(1), labels, text.T, image.T)
    return image_grad.T.astype(F32), text_grad.T.astype(F32)


def solution(mesh):
    return jax.shard_map(
        per_device,
        mesh=mesh,
        in_specs=(P("dp", "tower"), P("dp", "tower"), P(), P(), P(), P("dp", None)),
        out_specs=(P("dp", "tower"), P("dp", "tower")),
        check_vma=False,
    )
```

```python
from functools import partial

import jax
import jax.numpy as jnp
from jax import lax
from jax.experimental import pallas as pl
from jax.experimental.pallas import tpu as pltpu
from jax.sharding import PartitionSpec as P

MESH = pl.DeviceIdType.MESH
BF = jnp.bfloat16
F32 = jnp.float32
NT = (((1,), (1,)), ((), ()))
WIDTH, DEPTH, ROWS = 1152, 576, 1024
CHUNK, TILE = 256, 512
SLOT_OF_BIT = (5, 1, 2, 6, 3, 4)
NEAR = (1, 3, 5)
GATE = 5


def flip(index, bit):
    return index + (1 - 2 * ((index // (1 << bit)) % 2)) * (1 << bit)


def columns_of(half):
    return pl.ds(pl.multiple_of(DEPTH * half, DEPTH), DEPTH)


def rows_of(chunk):
    return pl.ds(CHUNK * chunk, CHUNK)


def kernel(
    table, scale_in, bias_in, labels_in, text_in, image_in, text_out, image_out,
    text_a, text_b, image_a, image_b, mine, q, kn, acc, gradient_out, labels, label_column,
    swap_s, swap_r, link_s, link_r, core_s, core_r, relay_s, last_s, last_r, label_s, label_r,
):
    me, a = lax.axis_index("dp"), lax.axis_index("tower")
    c = me % 2
    other = (c - a) * (c - a)
    sibling = (me + 1 - 2 * c, a)
    across = (me, 1 - a)
    diagonal = (me + 1 - 2 * c, 1 - a)
    home = (me - c + a, 1 - a)
    near = {1: (flip(me, 1), a), 3: (flip(me, 4), a), 5: across}
    beyond = {1: (flip(flip(me, 1), 2), a), 3: (flip(flip(me, 4), 5), a), 5: (flip(me, 3), 1 - a)}
    inputs, outputs = (text_in, image_in), (image_out, text_out)
    buffers = ((text_a, text_b), (image_a, image_b))

    barrier = pltpu.get_barrier_semaphore()
    peers = [sibling, across, diagonal, near[1], near[3], *beyond.values()]
    for peer in peers:
        pl.semaphore_signal(barrier, inc=1, device_id=peer, device_id_type=MESH)

    def remote(src, dst, send, recv, device):
        return pltpu.make_async_remote_copy(
            src_ref=src, dst_ref=dst, send_sem=send, recv_sem=recv, device_id=device, device_id_type=MESH
        )

    def place(slot, array, half, chunk):
        return buffers[array][chunk // 2].at[slot, columns_of(half), rows_of(chunk % 2)]

    def swap_copy(array, chunk):
        return remote(
            inputs[array].at[:, rows_of(chunk)], place(0, array, a, chunk),
            swap_s.at[array, chunk], swap_r.at[array, chunk], (me - c + a, c),
        )

    def swap_wait(array, chunk):
        remote(
            inputs[array].at[:, rows_of(chunk)], place(0, array, c, chunk),
            swap_s.at[array, chunk], swap_r.at[array, chunk], (me - c + a, c),
        ).wait_recv()

    def own_copy(array, chunk):
        return pltpu.make_async_copy(
            inputs[array].at[:, rows_of(chunk)], place(0, array, a, chunk), swap_r.at[array, chunk]
        )

    def beside_copy(array, chunk):
        return remote(
            inputs[array].at[:, rows_of(chunk)], place(5, array, a, chunk),
            link_s.at[2, array, chunk], link_r.at[4, array, chunk], sibling,
        )

    def link_copy(s, array, chunk):
        return remote(
            place(0, array, c, chunk), place(s, array, c, chunk),
            link_s.at[s // 2, array, chunk], link_r.at[s - 1, array, chunk], near[s],
        )

    def relay_copy(s, array, chunk):
        return remote(
            place(s, array, c, chunk), place(s + 1, array, c, chunk),
            relay_s.at[s // 2, array, chunk], link_r.at[s, array, chunk], beyond[s],
        )

    def core_copy(s, array, chunk, half):
        return remote(
            place(s, array, half, chunk), place(s, array, half, chunk),
            core_s.at[s, array, chunk], core_r.at[s, array, chunk], sibling,
        )

    def result(array, half, piece):
        return gradient_out.at[array, columns_of(half), rows_of(piece)]

    def landing(array, piece):
        row = pl.multiple_of(TILE * c + CHUNK * piece, CHUNK)
        return outputs[array].at[:, pl.ds(row, CHUNK)]

    def last_copy(array, half, piece, device):
        return remote(
            result(array, half, piece), landing(array, piece),
            last_s.at[array, half, piece], last_r.at[array, c, piece], device,
        )

    def home_copy(array, piece):
        return pltpu.make_async_copy(result(array, a, piece), landing(array, piece), last_r.at[array, c, piece])

    def pass_on(s, array, chunk):
        remote(
            place(0, array, c, chunk), place(s, array, c, chunk),
            link_s.at[0, array, chunk], link_r.at[s - 1, array, chunk], across,
        ).wait_recv()
        if s in NEAR:
            relay_copy(s, array, chunk).start()
        core_copy(s, array, chunk, c).start()

    def fan_out(array, chunk):
        link_copy(1, array, chunk).start()
        link_copy(3, array, chunk).start()
        core_copy(0, array, chunk, c).start()

    def pass_text(chunk):
        for s in (1, 3):
            pass_on(s, 0, chunk)
        if chunk > 1:
            for s in (2, 4):
                pass_on(s, 0, chunk - 2)

    chunks = [(array, chunk) for array in range(2) for chunk in range(4)]
    label_copy = remote(labels_in, labels, label_s, label_r, sibling)

    @pl.when(other == 0)
    def _():
        for which in chunks:
            own_copy(*which).start()

    pl.semaphore_wait(barrier, len(peers))

    @pl.when(other == 0)
    def _():
        label_copy.start()
        labels[...] = labels_in[...]
        for which in chunks:
            own_copy(*which).wait()
            fan_out(*which)
        label_copy.wait_send()

    @pl.when(other == 1)
    def _():
        for which in chunks:
            swap_copy(*which).start()
        for which in chunks:
            beside_copy(*which).start()
        label_copy.wait_recv()

    for b in range(4):
        row = labels[0:1, pl.ds(pl.multiple_of(512 * c + 128 * b, 128), 128)].astype(F32)
        label_column[0, 128 * b : 128 * b + 128, :] = jnp.broadcast_to(row, (128, 128)).T
    row = labels[0:1, :].astype(F32)
    position = lax.broadcasted_iota(jnp.int32, (8, 1024), 1).astype(F32)

    def invert(n, carry):
        base = (512 * c + 8 * n).astype(F32)
        this = lax.broadcasted_iota(jnp.int32, (8, 1024), 0).astype(F32) + base
        found = jnp.sum(jnp.where(row == this, position, 0.0), axis=1, keepdims=True)
        label_column[1, pl.ds(pl.multiple_of(8 * n, 8), 8), :] = jnp.broadcast_to(found, (8, 128))
        return carry

    lax.fori_loop(0, 64, invert, 0)

    def swapped_in(first, last):
        for n in range(first, last):
            swap_wait(*chunks[n])
            fan_out(*chunks[n])
            if n > 1:
                pass_on(6, *chunks[n - 2])
            if n % 2 == 1:
                pass_text(n // 2)

    @pl.when(other == 0)
    def _():
        for which in chunks:
            pass_on(5, *which)
        pass_text(0)
        pass_text(1)

    pl.when(other == 1)(partial(swapped_in, 0, 5))

    def inverse_norms(load):
        total = jnp.zeros((16, TILE), F32)
        for r in range(0, WIDTH, 16):
            part = load(r).astype(F32)
            total += part * part
        return lax.rsqrt(jnp.sum(total, axis=0, keepdims=True) + 1e-06)

    def normalise(load, k=0):
        inverse = inverse_norms(load)
        for r in range(0, WIDTH, 16):
            kn[k, r : r + 16, :] = (load(r).astype(F32) * inverse).astype(BF)

    def own_rows(array):
        for part in range(2):

            @pl.when(c == part)
            def _(part=part):
                mine[array] = buffers[array][part][0]

        normalise(lambda r: mine[array, r : r + 16, :])
        for b in range(0, WIDTH, 128):
            q[1 - array, :, b : b + 128] = kn[0, b : b + 128, :].astype(F32).T.astype(BF)

    for chunk in range(4):
        core_copy(0, 0, chunk, 1 - c).wait_recv()
    own_rows(0)

    @pl.when(other == 0)
    def _():
        pass_text(2)
        for n in range(4, 8):
            if n <= GATE:
                core_copy(0, *chunks[n], 1 - c).wait_recv()
        for first in chunks[: 7 - GATE]:
            link_copy(5, *first).start()
        for n in range(GATE + 1, 8):
            core_copy(0, *chunks[n], 1 - c).wait_recv()
        for which in chunks[7 - GATE :]:
            link_copy(5, *which).start()
        pass_text(3)

    @pl.when(other == 1)
    def _():
        swapped_in(5, 8)
        pass_on(6, *chunks[6])
        pass_on(6, *chunks[7])
        for n in range(4, 8):
            core_copy(0, *chunks[n], 1 - c).wait_recv()

    own_rows(1)
    acc[...] = jnp.zeros_like(acc)
    scale, bias = scale_in[0], bias_in[0]

    plan = {
        0: [((2, 4), 0, 2)],
        1: [((5,), 0, 0), ((1, 3), 1, 0)],
        2: [((5,), 0, 1)],
        3: [((2, 4), 0, 3), ((5,), 0, 2), ((6,), 0, 0)],
        4: [((1, 3), 1, 1), ((5,), 0, 3), ((6,), 0, 1)],
        5: [((5,), 1, 0), ((2, 4), 1, 0), ((6,), 0, 2)],
        6: [((1, 3), 1, 2)],
        7: [((5,), 1, 1), ((6,), 0, 3)],
        8: [((5,), 1, 2), ((2, 4), 1, 1)],
        9: [((1, 3), 1, 3), ((6,), 1, 0)],
        10: [((5,), 1, 3), ((6,), 1, 1)],
        11: [((2, 4), 1, 2), ((6,), 1, 2)],
        13: [((6,), 1, 3), ((2, 4), 1, 3)],
    }

    def hand_over(n):
        for several, array, chunk in plan.get(n, []):
            for s in several:
                if s == 5:
                    pl.when(other == 1)(partial(pass_on, s, array, chunk))
                elif s == 6:
                    pl.when(other == 0)(partial(pass_on, s, array, chunk))
                else:
                    pass_on(s, array, chunk)

    def finish(array, piece):
        rows = rows_of(piece)
        total = jnp.zeros((16, CHUNK), F32)
        square = jnp.zeros((16, CHUNK), F32)
        for r in range(0, WIDTH, 16):
            own = mine[1 - array, r : r + 16, rows].astype(F32)
            square += own * own
            total += own * acc[array, r : r + 16, rows]
        inverse = lax.rsqrt(jnp.sum(square, axis=0, keepdims=True) + 1e-06)
        along = jnp.sum(total, axis=0, keepdims=True) * inverse * scale
        first, second = inverse * scale, inverse * inverse * along
        for r in range(0, WIDTH, 16):
            unit_part = mine[1 - array, r : r + 16, rows].astype(F32) * second
            gradient_out[array, r : r + 16, rows] = (first * acc[array, r : r + 16, rows] - unit_part).astype(BF)
        last_copy(array, 1 - a, piece, home).start()

        @pl.when(other == 1)
        def _():
            last_copy(array, a, piece, sibling).start()

        @pl.when(other == 0)
        def _():
            home_copy(array, piece).start()

    def tile(array, part, own, k=0, first=0, size=TILE):
        rows = pl.ds(first, size)
        logits = jnp.dot(q[array, rows, :], kn[k], preferred_element_type=F32) * scale + bias
        weight = jax.nn.sigmoid(logits)
        if own:
            at = lax.broadcasted_iota(jnp.int32, (TILE, 128), 1).astype(F32) + float(TILE * part)
            column = label_column[array]
            positive = [jnp.where(column == at + 128.0 * u, 1.0, 0.0) for u in range(TILE // 128)]
            weight = weight - jnp.concatenate(positive, axis=1)
        acc[array, :, rows] += lax.dot_general(kn[k], weight.astype(BF), NT, preferred_element_type=F32)

    def slot_of(k):
        value = table[k, 0]
        return sum(jnp.where(value == 1 << b, s, 0) for b, s in enumerate(SLOT_OF_BIT))

    for n in range(4):
        array, part = n // 2, n % 2
        hand_over(n)
        normalise(lambda r, buffer=buffers[array][part]: buffer[0, r : r + 16, :])
        tile(array, part, True)

    for n in range(4):
        array, part = n // 2, n % 2
        buffer = buffers[array][part]
        hand_over(4 + 3 * n)
        for s in range(1, 7):
            for u in range(2):
                core_copy(s, array, 2 * part + u, 1 - c).wait_recv()

        if n == 3:
            for k in range(3):
                slot = slot_of(k)
                normalise(lambda r, slot=slot, buffer=buffer: buffer[slot, r : r + 16, :], k)
                tile(array, part, False, k, 0, CHUNK)
            finish(array, 0)
            for k in range(3):
                tile(array, part, False, k, CHUNK, CHUNK)
            finish(array, 1)
            continue

        def partner_tile(k, carry, n=n, array=array, part=part, buffer=buffer):
            for later in (1, 2):
                pl.when(k == later)(partial(hand_over, 4 + 3 * n + later))
            slot = slot_of(k)
            normalise(lambda r: buffer[slot, r : r + 16, :])
            tile(array, part, False)
            return carry

        lax.fori_loop(0, 3, partner_tile, 0)
        if n == 1:
            finish(array, 0)
            finish(array, 1)

    for array, chunk in chunks:
        for s in NEAR:
            link_copy(s, array, chunk).wait_send()
            relay_copy(s, array, chunk).wait_send()
        for s in range(7):
            core_copy(s, array, chunk, c).wait_send()

        @pl.when(other == 1)
        def _(array=array, chunk=chunk):
            swap_copy(array, chunk).wait_send()

    for array in range(2):
        for piece in range(2):
            for part in range(2):
                there = outputs[array].at[:, rows_of(2 * part + piece)]
                here = (1 - other) * (1 - (part - c) * (part - c))

                @pl.when(here == 1)
                def _(array=array, part=part, piece=piece, there=there):
                    pltpu.make_async_copy(result(array, 0, piece), there, last_r.at[array, part, piece]).wait()

                @pl.when(here == 0)
                def _(array=array, part=part, piece=piece, there=there):
                    remote(
                        result(array, 0, piece), there, last_s.at[array, 0, piece], last_r.at[array, part, piece], across
                    ).wait_recv()

            last_copy(array, 1 - a, piece, home).wait_send()

            @pl.when(other == 1)
            def _(array=array, piece=piece):
                last_copy(array, a, piece, sibling).wait_send()


def per_device(image, text, scale, bias, table, labels):
    dma = pltpu.SemaphoreType.DMA
    smem, vmem = pl.BlockSpec(memory_space=pltpu.SMEM), pl.BlockSpec(memory_space=pltpu.VMEM)
    anywhere = pl.BlockSpec(memory_space=pl.ANY)
    text_grad, image_grad = pl.pallas_call(
        kernel,
        out_shape=[jax.ShapeDtypeStruct((DEPTH, ROWS), BF)] * 2,
        in_specs=[smem, smem, smem, vmem, anywhere, anywhere],
        out_specs=[anywhere] * 2,
        scratch_shapes=[pltpu.VMEM((7, WIDTH, TILE), BF)] * 4
        + [
            pltpu.VMEM((2, WIDTH, TILE), BF),
            pltpu.VMEM((2, TILE, WIDTH), BF),
            pltpu.VMEM((3, WIDTH, TILE), BF),
            pltpu.VMEM((2, WIDTH, TILE), F32),
            pltpu.VMEM((2, WIDTH, TILE), BF),
            pltpu.VMEM((1, ROWS), jnp.int32),
            pltpu.VMEM((2, TILE, 128), F32),
            dma((2, 4)), dma((2, 4)), dma((3, 2, 4)), dma((6, 2, 4)), dma((7, 2, 4)), dma((7, 2, 4)), dma((3, 2, 4)),
            dma((2, 2, 2)), dma((2, 2, 2)), dma, dma,
        ],
        compiler_params=pltpu.CompilerParams(collective_id=0, has_side_effects=True, vmem_limit_bytes=58 * 2**20),
        cost_estimate=pl.CostEstimate(flops=20 * 10**9, bytes_accessed=6 * 10**6, transcendentals=4 * 2**20),
        name="rounds",
    )(table, scale.reshape(1), bias.reshape(1), labels, text.T, image.T)
    return image_grad.T.astype(F32), text_grad.T.astype(F32)


def solution(mesh):
    return jax.shard_map(
        per_device,
        mesh=mesh,
        in_specs=(P("dp", "tower"), P("dp", "tower"), P(), P(), P(), P("dp", None)),
        out_specs=(P("dp", "tower"), P("dp", "tower")),
        check_vma=False,
    )
```

```python
from functools import partial

import jax
import jax.numpy as jnp
from jax import lax
from jax.experimental import pallas as pl
from jax.experimental.pallas import tpu as pltpu
from jax.sharding import PartitionSpec as P

MESH = pl.DeviceIdType.MESH
BF = jnp.bfloat16
F32 = jnp.float32
NT = (((1,), (1,)), ((), ()))
WIDTH, DEPTH, ROWS = 1152, 576, 1024
CHUNK, TILE = 256, 512
SLOT_OF_BIT = (5, 1, 2, 6, 3, 4)
NEAR = (1, 3, 5)
GATE = 5


def flip(index, bit):
    return index + (1 - 2 * ((index // (1 << bit)) % 2)) * (1 << bit)


def columns_of(half):
    return pl.ds(pl.multiple_of(DEPTH * half, DEPTH), DEPTH)


def rows_of(chunk):
    return pl.ds(CHUNK * chunk, CHUNK)


def kernel(
    table, scale_in, bias_in, labels_in, text_in, image_in, text_out, image_out,
    text_a, text_b, image_a, image_b, mine, q, kn, acc, gradient_out, labels, label_column,
    swap_s, swap_r, link_s, link_r, core_s, core_r, relay_s, last_s, last_r, label_s, label_r,
):
    me, a = lax.axis_index("dp"), lax.axis_index("tower")
    c = me % 2
    other = (c - a) * (c - a)
    sibling = (me + 1 - 2 * c, a)
    across = (me, 1 - a)
    diagonal = (me + 1 - 2 * c, 1 - a)
    home = (me - c + a, 1 - a)
    near = {1: (flip(me, 1), a), 3: (flip(me, 4), a), 5: across}
    beyond = {1: (flip(flip(me, 1), 2), a), 3: (flip(flip(me, 4), 5), a), 5: (flip(me, 3), 1 - a)}
    inputs, outputs = (text_in, image_in), (image_out, text_out)
    buffers = ((text_a, text_b), (image_a, image_b))

    barrier = pltpu.get_barrier_semaphore()
    peers = [sibling, across, diagonal, near[1], near[3], *beyond.values()]
    for peer in peers:
        pl.semaphore_signal(barrier, inc=1, device_id=peer, device_id_type=MESH)

    def remote(src, dst, send, recv, device):
        return pltpu.make_async_remote_copy(
            src_ref=src, dst_ref=dst, send_sem=send, recv_sem=recv, device_id=device, device_id_type=MESH
        )

    def place(slot, array, half, chunk):
        return buffers[array][chunk // 2].at[slot, columns_of(half), rows_of(chunk % 2)]

    def swap_copy(array, chunk):
        return remote(
            inputs[array].at[:, rows_of(chunk)], place(0, array, a, chunk),
            swap_s.at[array, chunk], swap_r.at[array, chunk], (me - c + a, c),
        )

    def swap_wait(array, chunk):
        remote(
            inputs[array].at[:, rows_of(chunk)], place(0, array, c, chunk),
            swap_s.at[array, chunk], swap_r.at[array, chunk], (me - c + a, c),
        ).wait_recv()

    def own_copy(array, chunk):
        return pltpu.make_async_copy(
            inputs[array].at[:, rows_of(chunk)], place(0, array, a, chunk), swap_r.at[array, chunk]
        )

    def beside_copy(array, chunk):
        return remote(
            inputs[array].at[:, rows_of(chunk)], place(5, array, a, chunk),
            link_s.at[2, array, chunk], link_r.at[4, array, chunk], sibling,
        )

    def link_copy(s, array, chunk):
        return remote(
            place(0, array, c, chunk), place(s, array, c, chunk),
            link_s.at[s // 2, array, chunk], link_r.at[s - 1, array, chunk], near[s],
        )

    def relay_copy(s, array, chunk):
        return remote(
            place(s, array, c, chunk), place(s + 1, array, c, chunk),
            relay_s.at[s // 2, array, chunk], link_r.at[s, array, chunk], beyond[s],
        )

    def core_copy(s, array, chunk, half):
        return remote(
            place(s, array, half, chunk), place(s, array, half, chunk),
            core_s.at[s, array, chunk], core_r.at[s, array, chunk], sibling,
        )

    def result(array, half, piece):
        return gradient_out.at[array, columns_of(half), rows_of(piece)]

    def landing(array, piece):
        row = pl.multiple_of(TILE * c + CHUNK * piece, CHUNK)
        return outputs[array].at[:, pl.ds(row, CHUNK)]

    def last_copy(array, half, piece, device):
        return remote(
            result(array, half, piece), landing(array, piece),
            last_s.at[array, half, piece], last_r.at[array, c, piece], device,
        )

    def home_copy(array, piece):
        return pltpu.make_async_copy(result(array, a, piece), landing(array, piece), last_r.at[array, c, piece])

    def pass_on(s, array, chunk):
        remote(
            place(0, array, c, chunk), place(s, array, c, chunk),
            link_s.at[0, array, chunk], link_r.at[s - 1, array, chunk], across,
        ).wait_recv()
        if s in NEAR:
            relay_copy(s, array, chunk).start()
        core_copy(s, array, chunk, c).start()

    def fan_out(array, chunk):
        link_copy(1, array, chunk).start()
        link_copy(3, array, chunk).start()
        core_copy(0, array, chunk, c).start()

    def pass_text(chunk):
        for s in (1, 3):
            pass_on(s, 0, chunk)
        if chunk > 1:
            for s in (2, 4):
                pass_on(s, 0, chunk - 2)

    chunks = [(array, chunk) for array in range(2) for chunk in range(4)]
    label_copy = remote(labels_in, labels, label_s, label_r, sibling)

    @pl.when(other == 0)
    def _():
        for which in chunks:
            own_copy(*which).start()

    pl.semaphore_wait(barrier, len(peers))

    @pl.when(other == 0)
    def _():
        label_copy.start()
        labels[...] = labels_in[...]
        for which in chunks:
            own_copy(*which).wait()
            fan_out(*which)
        label_copy.wait_send()

    @pl.when(other == 1)
    def _():
        for which in chunks:
            swap_copy(*which).start()
        for which in chunks:
            beside_copy(*which).start()
        label_copy.wait_recv()

    for b in range(4):
        row = labels[0:1, pl.ds(pl.multiple_of(512 * c + 128 * b, 128), 128)].astype(F32)
        label_column[0, 128 * b : 128 * b + 128, :] = jnp.broadcast_to(row, (128, 128)).T
    row = labels[0:1, :].astype(F32)
    position = lax.broadcasted_iota(jnp.int32, (8, 1024), 1).astype(F32)

    def invert(n, carry):
        base = (512 * c + 8 * n).astype(F32)
        this = lax.broadcasted_iota(jnp.int32, (8, 1024), 0).astype(F32) + base
        found = jnp.sum(jnp.where(row == this, position, 0.0), axis=1, keepdims=True)
        label_column[1, pl.ds(pl.multiple_of(8 * n, 8), 8), :] = jnp.broadcast_to(found, (8, 128))
        return carry

    lax.fori_loop(0, 64, invert, 0)

    def swapped_in(first, last):
        for n in range(first, last):
            swap_wait(*chunks[n])
            fan_out(*chunks[n])
            if n > 1:
                pass_on(6, *chunks[n - 2])
            if n % 2 == 1:
                pass_text(n // 2)

    @pl.when(other == 0)
    def _():
        for which in chunks:
            pass_on(5, *which)
        pass_text(0)
        pass_text(1)

    pl.when(other == 1)(partial(swapped_in, 0, 5))

    def inverse_norms(load):
        total = jnp.zeros((16, TILE), F32)
        for r in range(0, WIDTH, 16):
            part = load(r).astype(F32)
            total += part * part
        return lax.rsqrt(jnp.sum(total, axis=0, keepdims=True) + 1e-06)

    def normalise(load, k=0):
        inverse = inverse_norms(load)
        for r in range(0, WIDTH, 16):
            kn[k, r : r + 16, :] = (load(r).astype(F32) * inverse).astype(BF)

    def own_rows(array):
        for part in range(2):

            @pl.when(c == part)
            def _(part=part):
                mine[array] = buffers[array][part][0]

        normalise(lambda r: mine[array, r : r + 16, :])
        for b in range(0, WIDTH, 128):
            q[1 - array, :, b : b + 128] = kn[0, b : b + 128, :].astype(F32).T.astype(BF)

    for chunk in range(4):
        core_copy(0, 0, chunk, 1 - c).wait_recv()
    own_rows(0)

    @pl.when(other == 0)
    def _():
        pass_text(2)
        for n in range(4, 8):
            if n <= GATE:
                core_copy(0, *chunks[n], 1 - c).wait_recv()
        for first in chunks[: 7 - GATE]:
            link_copy(5, *first).start()
        for n in range(GATE + 1, 8):
            core_copy(0, *chunks[n], 1 - c).wait_recv()
        for which in chunks[7 - GATE :]:
            link_copy(5, *which).start()
        pass_text(3)

    @pl.when(other == 1)
    def _():
        swapped_in(5, 8)
        pass_on(6, *chunks[6])
        pass_on(6, *chunks[7])
        for n in range(4, 8):
            core_copy(0, *chunks[n], 1 - c).wait_recv()

    own_rows(1)
    acc[...] = jnp.zeros_like(acc)
    scale, bias = scale_in[0], bias_in[0]

    plan = {
        0: [((2, 4), 0, 2)],
        1: [((5,), 0, 0), ((1, 3), 1, 0)],
        2: [((5,), 0, 1)],
        3: [((5,), 0, 2), ((2, 4), 0, 3), ((6,), 0, 0)],
        4: [((1, 3), 1, 1), ((5,), 0, 3), ((6,), 0, 1), ((5,), 1, 0)],
        5: [((2, 4), 1, 0), ((6,), 0, 2)],
        6: [((1, 3), 1, 2), ((5,), 1, 1)],
        7: [((6,), 0, 3)],
        8: [((5,), 1, 2), ((2, 4), 1, 1)],
        9: [((1, 3), 1, 3), ((5,), 1, 3), ((6,), 1, 0)],
        10: [((6,), 1, 1)],
        11: [((2, 4), 1, 2), ((6,), 1, 2)],
        13: [((6,), 1, 3), ((2, 4), 1, 3)],
    }

    def hand_over(n):
        for several, array, chunk in plan.get(n, []):
            for s in several:
                if s == 5:
                    pl.when(other == 1)(partial(pass_on, s, array, chunk))
                elif s == 6:
                    pl.when(other == 0)(partial(pass_on, s, array, chunk))
                else:
                    pass_on(s, array, chunk)

    def finish(array, piece):
        rows = rows_of(piece)
        total = jnp.zeros((16, CHUNK), F32)
        square = jnp.zeros((16, CHUNK), F32)
        for r in range(0, WIDTH, 16):
            own = mine[1 - array, r : r + 16, rows].astype(F32)
            square += own * own
            total += own * acc[array, r : r + 16, rows]
        inverse = lax.rsqrt(jnp.sum(square, axis=0, keepdims=True) + 1e-06)
        along = jnp.sum(total, axis=0, keepdims=True) * inverse * scale
        first, second = inverse * scale, inverse * inverse * along
        for r in range(0, WIDTH, 16):
            unit_part = mine[1 - array, r : r + 16, rows].astype(F32) * second
            gradient_out[array, r : r + 16, rows] = (first * acc[array, r : r + 16, rows] - unit_part).astype(BF)
        last_copy(array, 1 - a, piece, home).start()

        @pl.when(other == 1)
        def _():
            last_copy(array, a, piece, sibling).start()

        @pl.when(other == 0)
        def _():
            home_copy(array, piece).start()

    def tile(array, part, own, k=0, first=0, size=TILE):
        rows = pl.ds(first, size)
        logits = jnp.dot(q[array, rows, :], kn[k], preferred_element_type=F32) * scale + bias
        weight = jax.nn.sigmoid(logits)
        if own:
            at = lax.broadcasted_iota(jnp.int32, (TILE, 128), 1).astype(F32) + float(TILE * part)
            column = label_column[array]
            positive = [jnp.where(column == at + 128.0 * u, 1.0, 0.0) for u in range(TILE // 128)]
            weight = weight - jnp.concatenate(positive, axis=1)
        acc[array, :, rows] += lax.dot_general(kn[k], weight.astype(BF), NT, preferred_element_type=F32)

    def slot_of(k):
        value = table[k, 0]
        return sum(jnp.where(value == 1 << b, s, 0) for b, s in enumerate(SLOT_OF_BIT))

    for n in range(4):
        array, part = n // 2, n % 2
        hand_over(n)
        normalise(lambda r, buffer=buffers[array][part]: buffer[0, r : r + 16, :])
        tile(array, part, True)

    for n in range(4):
        array, part = n // 2, n % 2
        buffer = buffers[array][part]
        hand_over(4 + 3 * n)
        for s in range(1, 7):
            for u in range(2):
                core_copy(s, array, 2 * part + u, 1 - c).wait_recv()

        if n == 3:
            for k in range(3):
                slot = slot_of(k)
                normalise(lambda r, slot=slot, buffer=buffer: buffer[slot, r : r + 16, :], k)
                tile(array, part, False, k, 0, CHUNK)
            finish(array, 0)
            for k in range(3):
                tile(array, part, False, k, CHUNK, CHUNK)
            finish(array, 1)
            continue

        def partner_tile(k, carry, n=n, array=array, part=part, buffer=buffer):
            for later in (1, 2):
                pl.when(k == later)(partial(hand_over, 4 + 3 * n + later))
            slot = slot_of(k)
            normalise(lambda r: buffer[slot, r : r + 16, :])
            tile(array, part, False)
            return carry

        lax.fori_loop(0, 3, partner_tile, 0)
        if n == 1:
            finish(array, 0)
            finish(array, 1)

    for array, chunk in chunks:
        for s in NEAR:
            link_copy(s, array, chunk).wait_send()
            relay_copy(s, array, chunk).wait_send()
        for s in range(7):
            core_copy(s, array, chunk, c).wait_send()

        @pl.when(other == 1)
        def _(array=array, chunk=chunk):
            swap_copy(array, chunk).wait_send()

    for array in range(2):
        for piece in range(2):
            for part in range(2):
                there = outputs[array].at[:, rows_of(2 * part + piece)]
                here = (1 - other) * (1 - (part - c) * (part - c))

                @pl.when(here == 1)
                def _(array=array, part=part, piece=piece, there=there):
                    pltpu.make_async_copy(result(array, 0, piece), there, last_r.at[array, part, piece]).wait()

                @pl.when(here == 0)
                def _(array=array, part=part, piece=piece, there=there):
                    remote(
                        result(array, 0, piece), there, last_s.at[array, 0, piece], last_r.at[array, part, piece], across
                    ).wait_recv()

            last_copy(array, 1 - a, piece, home).wait_send()

            @pl.when(other == 1)
            def _(array=array, piece=piece):
                last_copy(array, a, piece, sibling).wait_send()


def per_device(image, text, scale, bias, table, labels):
    dma = pltpu.SemaphoreType.DMA
    smem, vmem = pl.BlockSpec(memory_space=pltpu.SMEM), pl.BlockSpec(memory_space=pltpu.VMEM)
    anywhere = pl.BlockSpec(memory_space=pl.ANY)
    text_grad, image_grad = pl.pallas_call(
        kernel,
        out_shape=[jax.ShapeDtypeStruct((DEPTH, ROWS), BF)] * 2,
        in_specs=[smem, smem, smem, vmem, anywhere, anywhere],
        out_specs=[anywhere] * 2,
        scratch_shapes=[pltpu.VMEM((7, WIDTH, TILE), BF)] * 4
        + [
            pltpu.VMEM((2, WIDTH, TILE), BF),
            pltpu.VMEM((2, TILE, WIDTH), BF),
            pltpu.VMEM((3, WIDTH, TILE), BF),
            pltpu.VMEM((2, WIDTH, TILE), F32),
            pltpu.VMEM((2, WIDTH, TILE), BF),
            pltpu.VMEM((1, ROWS), jnp.int32),
            pltpu.VMEM((2, TILE, 128), F32),
            dma((2, 4)), dma((2, 4)), dma((3, 2, 4)), dma((6, 2, 4)), dma((7, 2, 4)), dma((7, 2, 4)), dma((3, 2, 4)),
            dma((2, 2, 2)), dma((2, 2, 2)), dma, dma,
        ],
        compiler_params=pltpu.CompilerParams(collective_id=0, has_side_effects=True, vmem_limit_bytes=58 * 2**20),
        cost_estimate=pl.CostEstimate(flops=20 * 10**9, bytes_accessed=6 * 10**6, transcendentals=4 * 2**20),
        name="rounds",
    )(table, scale.reshape(1), bias.reshape(1), labels, text.T, image.T)
    return image_grad.T.astype(F32), text_grad.T.astype(F32)


def solution(mesh):
    return jax.shard_map(
        per_device,
        mesh=mesh,
        in_specs=(P("dp", "tower"), P("dp", "tower"), P(), P(), P(), P("dp", None)),
        out_specs=(P("dp", "tower"), P("dp", "tower")),
        check_vma=False,
    )
```
